32 devices in a mesh: row: 4 (over y, x), col: 8 (over z, core).
Axes of the slice: x: 2, y: 2, z: 4, core: 2. Of those that a mesh axis runs over, the one named last changes fastest.
Arguments:
- density: bfloat16 [8192, 8192], P('col', 'row'), may hold values from -1 to 1
- pattern_p: int32 [64, 64], replicated, may hold values 0 or 1
- pattern_square: int32 [64, 64], replicated, may hold values 0 or 1
- pattern_cube: int32 [64, 64], replicated, may hold values 0 or 1
Outputs:
- purified: float32 [8192, 8192], P('col', 'row')
The draws below stay inside these ranges and needn't reach their ends.
All inputs are finite; a program needn't handle non-finite values.
Results may differ from the reference program's by a relative error of at most 0.009.
Values may be sent and summed in bfloat16 or wider, within the bound.
No kernel may reach another device: no remote copies, remote signals or barrier semaphores. Data moves between devices by JAX's collectives and lax.ppermute only.
A program may use at most 128 MiB of HBM per device.

```python
import jax
import jax.numpy as jnp

TILE = 128
N = 8192
NT = 64


def draw_density(key, part):
    scale = 0.9 * (N / 2.0) ** (-0.3)
    values = jax.random.normal(key, (N, N), jnp.float32)
    return jnp.clip(values * scale, -1.0, 1.0).astype(jnp.bfloat16)


def touch_ends(array, rng, least, top_value):
    longest = array.shape.index(max(array.shape))
    spots = []
    for shift in (0, 1):
        where = [jax.random.randint(jax.random.fold_in(rng, axis), (), 0, length) for axis, length in enumerate(array.shape)]
        where[longest] = (where[longest] + shift) % array.shape[longest]
        spots.append(tuple(where))
    return array.at[spots[0]].set(least).at[spots[1]].set(top_value)


def setup_inputs(seed: int = 0) -> dict:
    seeds = jax.random.split(jax.random.key(seed), 5)
    return {
        "density": draw_density(jax.random.fold_in(seeds[4], 71), 0),
        "pattern_p": touch_ends((jax.random.randint(seeds[1], (NT, NT), 0, 2) < 1).astype(jnp.int32), jax.random.fold_in(seeds[1], 1), 0, 1),
        "pattern_square": touch_ends((jax.random.randint(seeds[2], (NT, NT), 0, 2) < 1).astype(jnp.int32), jax.random.fold_in(seeds[2], 1), 0, 1),
        "pattern_cube": touch_ends((jax.random.randint(seeds[3], (NT, NT), 0, 2) < 1).astype(jnp.int32), jax.random.fold_in(seeds[3], 1), 0, 1),
    }


def expand(pattern):
    return jnp.repeat(jnp.repeat(pattern, TILE, 0), TILE, 1)


def reference(density, pattern_p, pattern_square, pattern_cube):
    masked = density * expand(pattern_p).astype(jnp.bfloat16)
    square = jnp.dot(masked, masked, preferred_element_type=jnp.float32)
    square_low = square.astype(jnp.bfloat16)
    cube = jnp.dot(square_low, masked, preferred_element_type=jnp.float32)
    keep_square = expand(pattern_square).astype(jnp.float32)
    keep_cube = expand(pattern_cube).astype(jnp.float32)
    return 3.0 * keep_square * square - 2.0 * keep_cube * cube
```

```python
import functools
import math

import jax
import jax.numpy as jnp
import numpy as np
from jax import lax
from jax.experimental import pallas as pl
from jax.experimental.pallas import tpu as pltpu
from jax.sharding import PartitionSpec as P

TILE = 128
ROW_GROUP = 4
WIDTHS = (4, 4, 4, 4)
DEPTH = 1024
VMEM_BYTES = 60 * 2**20
SMEM = pl.BlockSpec(memory_space=pltpu.SMEM)
VMEM = pl.BlockSpec(memory_space=pltpu.VMEM)
ANY = pl.BlockSpec(memory_space=pl.ANY)


def tile_mask(pattern, row_start, col_start, nrows, ncols):
    tile_rows = nrows // TILE + 2
    tile_cols = ncols // TILE + 2
    padded = jnp.pad(pattern, ((0, tile_rows), (0, tile_cols)))
    block = lax.dynamic_slice(
        padded, (row_start // TILE, col_start // TILE), (tile_rows, tile_cols)
    )
    spread = jnp.repeat(jnp.repeat(block, TILE, 0), TILE, 1)
    return lax.dynamic_slice(spread, (row_start % TILE, col_start % TILE), (nrows, ncols))


def dense_step(density, pattern_p, pattern_square, pattern_cube):
    nrows, ncols = density.shape
    row_start = lax.axis_index("col") * nrows
    col_start = lax.axis_index("row") * ncols
    masked = density * tile_mask(pattern_p, row_start, col_start, nrows, ncols).astype(jnp.bfloat16)
    column_panel = lax.all_gather(masked, "col", axis=0, tiled=True)

    def right_fold(piece):
        return jnp.dot(piece, column_panel, preferred_element_type=jnp.float32)

    square = right_fold(lax.all_gather(masked, "row", axis=1, tiled=True))
    cube = right_fold(lax.all_gather(square.astype(jnp.bfloat16), "row", axis=1, tiled=True))
    keep_square = tile_mask(pattern_square, row_start, col_start, nrows, ncols).astype(jnp.float32)
    keep_cube = tile_mask(pattern_cube, row_start, col_start, nrows, ncols).astype(jnp.float32)
    return 3.0 * keep_square * square - 2.0 * keep_cube * cube


def chunk_bounds(tile_rows, widths):
    bounds, cols = [], 0
    for width in widths:
        cols += width
        tiles = tile_rows * cols
        sigmas = 3.6 if cols == sum(widths) else 4.2
        bounds.append(min(tiles, 2 * math.ceil((tiles + sigmas * math.sqrt(tiles)) / 4)))
    return [min(b, bounds[-1]) for b in bounds]


def slot_table(pattern, tile_rows, tile_cols):
    n = pattern.shape[0]
    at = np.arange(n)
    same_rows = at[:, None] // tile_rows == at[None, :] // tile_rows
    above = (same_rows & (at[None, :] < at[:, None])).astype(np.float32)
    same_cols = at[:, None] // tile_cols == at[None, :] // tile_cols
    left = (same_cols & (at[:, None] < at[None, :])).astype(np.float32)
    kept = pattern.astype(jnp.bfloat16)
    dot = functools.partial(jnp.dot, preferred_element_type=jnp.float32)
    in_column = dot(jnp.asarray(above, jnp.bfloat16), kept)
    column = dot(jnp.asarray(same_rows, jnp.bfloat16), kept).astype(jnp.bfloat16)
    before = dot(column, jnp.asarray(left, jnp.bfloat16))
    return jnp.where(pattern != 0, (in_column + before).astype(jnp.int32), -1)


def tile_at(ref, i, j):
    return ref.at[pl.ds(pl.multiple_of(i * TILE, TILE), TILE), pl.ds(pl.multiple_of(j * TILE, TILE), TILE)]


def send_kept(table_ref, place_ref, x_ref, outs, sems, spans, shape):
    tile_rows, tile_cols = shape
    c, r = place_ref[0], place_ref[1]

    def send(i, j, slot):
        for q, (lo, hi) in enumerate(spans):
            @pl.when((slot >= lo) & (slot < hi))
            def _():
                pltpu.make_async_copy(tile_at(x_ref, i, j), outs[q].at[slot - lo], sems.at[q]).start()

    def step(n, used):
        j, i = n // tile_rows, n % tile_rows
        slot = table_ref[c * tile_rows + i, r * tile_cols + j]
        send(i, j, slot)
        return used + (slot >= 0).astype(jnp.int32)

    used = lax.fori_loop(0, tile_rows * tile_cols, step, jnp.int32(0))
    top = max(hi for _, hi in spans)

    def fill(slot, z):
        send(0, 0, slot)
        return z

    lax.fori_loop(used, jnp.int32(top), fill, 0)
    for q, out in enumerate(outs):
        pltpu.make_async_copy(out, out, sems.at[q]).wait()


def pack(table, place, density, spans):
    shape = density.shape[0] // TILE, density.shape[1] // TILE

    def kernel(table_ref, place_ref, x_ref, *refs):
        send_kept(table_ref, place_ref, x_ref, refs[:-1], refs[-1], spans, shape)

    return pl.pallas_call(
        kernel,
        out_shape=[jax.ShapeDtypeStruct((hi - lo, TILE, TILE), density.dtype) for lo, hi in spans],
        in_specs=[SMEM, SMEM, VMEM],
        out_specs=[ANY] * len(spans),
        scratch_shapes=[pltpu.SemaphoreType.DMA((len(spans),))],
        name="pack",
    )(table, place, density)


def stage(halves, lo, hi, after):
    cut = halves[0].shape[0]
    parts = []
    if lo < cut:
        parts.append((0, lo, min(hi, cut)))
    if hi > cut:
        parts.append((1, max(lo, cut) - cut, hi - cut))

    def kernel(h0, h1, after_ref, out, sem):
        at, copies = 0, []
        for which, first, end in parts:
            src = (h0, h1)[which].at[pl.ds(first, end - first)]
            copies.append(pltpu.make_async_copy(src, out.at[pl.ds(at, end - first)], sem.at[which]))
            at += end - first
        for copy in copies:
            copy.start()
        for copy in copies:
            copy.wait()

    return pl.pallas_call(
        kernel,
        out_shape=jax.ShapeDtypeStruct((hi - lo, TILE, TILE), halves[0].dtype),
        in_specs=[ANY, ANY, ANY],
        out_specs=VMEM,
        scratch_shapes=[pltpu.SemaphoreType.DMA((2,))],
        name="stage",
    )(*halves, after)


def row_unpack(table, place, density, pieces, widths):
    nrows, ncols = density.shape
    tile_rows, tile_cols = nrows // TILE, ncols // TILE
    n_tiles = table.shape[0]
    halves = [x.shape[0] for x in pieces[0]]
    flat = [x for piece in pieces for x in piece]

    def kernel(table_ref, place_ref, x_ref, *refs):
        ins, (out, held, sems) = refs[:-3], refs[-3:]
        i = pl.program_id(0)
        c, r = place_ref[0], place_ref[1]

        @pl.when(i == 0)
        def _():
            copies = []
            for n, ref in enumerate(ins):
                k, which = divmod(n, 2)
                target = held.at[k, pl.ds(which * halves[0], halves[which])]
                copies.append(pltpu.make_async_copy(ref, target, sems.at[n]))
            for copy in copies:
                copy.start()
            for copy in copies:
                copy.wait()

        d = first = 0
        for width in widths:
            for k in range(ROW_GROUP):
                for t in range(width):
                    j = first + t
                    slot = table_ref[c * tile_rows + i, (r ^ k) * tile_cols + j]
                    if k == 0:
                        tile = x_ref[:, j * TILE : (j + 1) * TILE]
                    else:
                        tile = held[k - 1, jnp.maximum(slot, 0)]
                    out[:, d * TILE : (d + 1) * TILE] = jnp.where(slot >= 0, tile, jnp.zeros_like(tile))
                    d += 1
            first += width

    return pl.pallas_call(
        kernel,
        grid=(tile_rows,),
        out_shape=jax.ShapeDtypeStruct((nrows, n_tiles * TILE), jnp.bfloat16),
        in_specs=[SMEM, SMEM, pl.BlockSpec((TILE, ncols), lambda i: (i, 0))] + [ANY] * len(flat),
        out_specs=pl.BlockSpec((TILE, n_tiles * TILE), lambda i: (i, 0)),
        scratch_shapes=[
            pltpu.VMEM((len(pieces), sum(halves), TILE, TILE), jnp.bfloat16),
            pltpu.SemaphoreType.DMA((len(flat),)),
        ],
        compiler_params=pltpu.CompilerParams(vmem_limit_bytes=VMEM_BYTES),
        name="row_unpack",
    )(table, place, density, *flat)


def square_group(table, place, row_panel, chunks, spans, h, widths, shape):
    tile_rows, tile_cols = shape
    nrows, depth = row_panel.shape
    n = widths[h] * TILE
    blocks = depth // DEPTH
    block_tiles = DEPTH // TILE
    first_h = sum(widths[:h])
    order = []
    first = 0
    for width in widths:
        order += [(k, first + t) for k in range(ROW_GROUP) for t in range(width)]
        first += width

    def kernel(table_ref, place_ref, a_ref, *refs):
        ins, (panel_out, square, top, bottom, a, panel, a_sems, sems, out_sem) = refs[: len(chunks)], refs[len(chunks) :]
        c, r = place_ref[0], place_ref[1]

        def a_copy(b):
            lanes = pl.ds(pl.multiple_of(b * DEPTH, DEPTH), DEPTH)
            return pltpu.make_async_copy(a_ref.at[:, lanes], a.at[:, lanes], a_sems.at[b])

        def out_copy(b):
            rows = pl.ds(pl.multiple_of(b * DEPTH, DEPTH), DEPTH)
            return pltpu.make_async_copy(panel.at[rows], panel_out.at[rows], out_sem)

        for b in range(blocks):
            a_copy(b).start()
        panel[...] = jnp.zeros_like(panel)
        for b in range(blocks):
            for d in range(b * block_tiles, (b + 1) * block_tiles):
                k, t = order[d]
                i = (r ^ k) * tile_cols + t
                owner = i // tile_rows
                for j in range(widths[h]):
                    slot = table_ref[i, r * tile_cols + first_h + j]
                    target = panel.at[d * TILE : (d + 1) * TILE, j * TILE : (j + 1) * TILE]
                    for q, (lo, hi) in enumerate(spans[: h + 1]):
                        @pl.when((slot >= lo) & (slot < hi))
                        def _():
                            source = ins[q].at[owner * (hi - lo) + slot - lo]
                            pltpu.make_async_copy(source, target, sems.at[b]).start()
        for b in range(blocks):
            for d in range(b * block_tiles, (b + 1) * block_tiles):
                k, t = order[d]
                for j in range(widths[h]):
                    target = panel.at[d * TILE : (d + 1) * TILE, j * TILE : (j + 1) * TILE]

                    @pl.when(table_ref[(r ^ k) * tile_cols + t, r * tile_cols + first_h + j] >= 0)
                    def _():
                        pltpu.make_async_copy(target, target, sems.at[b]).wait()

        def step(b, z):
            a_copy(b).wait()
            out_copy(b).start()
            at = pl.ds(pl.multiple_of(b * DEPTH, DEPTH), DEPTH)
            part = jnp.dot(a[:, at], panel[at, :], preferred_element_type=jnp.float32)

            @pl.when(b == 0)
            def _():
                square[...] = part

            @pl.when(b > 0)
            def _():
                square[...] += part

            return z

        lax.fori_loop(0, blocks, step, 0)
        top[...] = square[: nrows // 2].astype(jnp.bfloat16)
        bottom[...] = square[nrows // 2 :].astype(jnp.bfloat16)
        for b in range(blocks):
            out_copy(b).wait()

    half = jax.ShapeDtypeStruct((nrows // 2, n), jnp.bfloat16)
    return pl.pallas_call(
        kernel,
        out_shape=[
            jax.ShapeDtypeStruct((depth, n), jnp.bfloat16), jax.ShapeDtypeStruct((nrows, n), jnp.float32), half, half,
        ],
        in_specs=[SMEM, SMEM, ANY] + [ANY] * len(chunks),
        out_specs=[ANY, VMEM, VMEM, VMEM],
        scratch_shapes=[
            pltpu.VMEM((nrows, depth), jnp.bfloat16),
            pltpu.VMEM((depth, n), jnp.bfloat16),
            pltpu.SemaphoreType.DMA((blocks,)),
            pltpu.SemaphoreType.DMA((blocks,)),
            pltpu.SemaphoreType.DMA,
        ],
        compiler_params=pltpu.CompilerParams(vmem_limit_bytes=VMEM_BYTES),
        cost_estimate=pl.CostEstimate(
            flops=2 * nrows * depth * n, bytes_accessed=2 * depth * (nrows + 2 * n) + 6 * nrows * n, transcendentals=0
        ),
        name="square_group",
    )(table, place, row_panel, *chunks)


def cube_part(strips, panels, lo, widths, before=None, finish=None):
    half = strips[0][0][0].shape[0]
    nrows = 2 * half
    sizes = [group[0][0].shape[1] for group in strips]
    depth = ROW_GROUP * sum(sizes)
    blocks = depth // DEPTH
    total = sum(widths) * TILE
    lefts, at = [], 0
    for group, size in zip(strips, sizes):
        for pair in group:
            lefts += [(pair[0], 0, at, size), (pair[1], half, at, size)]
            at += size
    widest = max(widths) * TILE
    firsts = [sum(widths[:h]) for h in range(len(widths))]
    n_left, n_panels = len(lefts), len(panels)
    operands = [x for x, *_ in lefts] + list(panels)
    specs = [ANY] * len(operands)
    if before is not None:
        operands.append(before)
        specs.append(ANY)
    if finish is not None:
        place, pattern_square, pattern_cube, squares = finish
        operands += [place, pattern_square, pattern_cube, *squares]
        specs += [SMEM] * 3 + [ANY] * len(squares)

    def kernel(*refs):
        left_refs, refs = refs[:n_left], refs[n_left:]
        panel_refs, refs = refs[:n_panels], refs[n_panels:]
        if before is not None:
            before_ref, refs = refs[0], refs[1:]
        if finish is not None:
            (place_ref, keep_square, keep_cube), refs = refs[:3], refs[3:]
            square_refs, refs = refs[:n_panels], refs[n_panels:]
        out, left, right, acc, held, left_sem, right_sems, acc_sems, held_sems, out_sems = refs

        def loads(h):
            s, n = h % 2, widths[h] * TILE
            copies = [pltpu.make_async_copy(panel_refs[h].at[pl.ds(lo, depth)], right.at[s, :, :n], right_sems.at[s])]
            if before is not None:
                lanes = pl.ds(firsts[h] * TILE, n)
                copies.append(pltpu.make_async_copy(before_ref.at[:, lanes], acc.at[s, :, :n], acc_sems.at[s]))
            if finish is not None:
                copies.append(pltpu.make_async_copy(square_refs[h], held.at[s, :, :n], held_sems.at[s]))
            return copies

        def store(h):
            s, n = h % 2, widths[h] * TILE
            lanes = pl.ds(firsts[h] * TILE, n)
            source = held if finish is not None else acc
            return pltpu.make_async_copy(source.at[s, :, :n], out.at[:, lanes], out_sems.at[s])

        left_copies = [
            pltpu.make_async_copy(ref, left.at[pl.ds(row, half), pl.ds(col, size)], left_sem.at[0])
            for ref, (_, row, col, size) in zip(left_refs, lefts)
        ]
        for copy in left_copies + loads(0):
            copy.start()
        for copy in left_copies:
            copy.wait()
        for h in range(n_panels):
            s, n = h % 2, widths[h] * TILE
            if h >= 1:
                store(h - 1).wait()
            if h + 1 < n_panels:
                for copy in loads(h + 1):
                    copy.start()
            for copy in loads(h):
                copy.wait()

            def step(b, z):
                at = pl.ds(pl.multiple_of(b * DEPTH, DEPTH), DEPTH)
                part = jnp.dot(left[:, at], right[s, at, :n], preferred_element_type=jnp.float32)
                if before is None:
                    @pl.when(b == 0)
                    def _():
                        acc[s, :, :n] = part

                    @pl.when(b > 0)
                    def _():
                        acc[s, :, :n] += part
                else:
                    acc[s, :, :n] += part
                return z

            lax.fori_loop(0, blocks, step, 0)
            if finish is not None:
                tile_rows, tile_cols = nrows // TILE, total // TILE
                row, col = place_ref[0] * tile_rows, place_ref[1] * tile_cols + firsts[h]

                def combine(i, z):
                    rows = pl.ds(pl.multiple_of(i * TILE, TILE), TILE)
                    for j in range(widths[h]):
                        lanes = slice(j * TILE, (j + 1) * TILE)
                        a = 3.0 * keep_square[row + i, col + j].astype(jnp.float32)
                        b = 2.0 * keep_cube[row + i, col + j].astype(jnp.float32)
                        held[s, rows, lanes] = a * held[s, rows, lanes] - b * acc[s, rows, lanes]
                    return z

                lax.fori_loop(0, tile_rows, combine, 0)
            store(h).start()
        store(n_panels - 1).wait()

    return pl.pallas_call(
        kernel,
        out_shape=jax.ShapeDtypeStruct((nrows, total), jnp.float32),
        in_specs=specs,
        out_specs=ANY,
        scratch_shapes=[
            pltpu.VMEM((nrows, depth), jnp.bfloat16),
            pltpu.VMEM((2, depth, widest), jnp.bfloat16),
            pltpu.VMEM((2, nrows, widest), jnp.float32),
            pltpu.VMEM((2, nrows, widest) if finish is not None else (2, 8, TILE), jnp.float32),
            pltpu.SemaphoreType.DMA((1,)),
            pltpu.SemaphoreType.DMA((2,)),
            pltpu.SemaphoreType.DMA((2,)),
            pltpu.SemaphoreType.DMA((2,)),
            pltpu.SemaphoreType.DMA((2,)),
        ],
        compiler_params=pltpu.CompilerParams(vmem_limit_bytes=VMEM_BYTES),
        cost_estimate=pl.CostEstimate(
            flops=2 * nrows * depth * total, bytes_accessed=2 * depth * total + 8 * nrows * total, transcendentals=0
        ),
        name="cube_part",
    )(*operands)


def packed_step(density, table, place, pattern_square, pattern_cube, packed, spans, widths):
    shape = density.shape[0] // TILE, density.shape[1] // TILE
    *halves, first_chunk = packed

    def swap(x, k):
        return lax.ppermute(x, "row", [(i, i ^ k) for i in range(ROW_GROUP)])

    def exchange(top, bottom):
        by_x = swap(top, 1), swap(bottom, 1)
        by_y = swap(top, 2), swap(bottom, 2)
        far = swap(by_x[0], 2), swap(by_y[1], 1)
        return by_x, by_y, far

    def gather(x):
        return lax.all_gather(x, "col", axis=0, tiled=True)

    pieces = exchange(*halves)
    chunks = [gather(first_chunk)]
    chunks.append(gather(stage(halves, *spans[1], pieces[0][0])))
    chunks.append(gather(stage(halves, *spans[2], pieces[2][0])))
    row_panel = row_unpack(table, place, density, pieces, widths)

    panels, squares, strips = [], [], []
    for h in range(len(widths)):
        if h == 1:
            chunks.append(gather(stage(halves, *spans[3], strips[0][0][0])))
        panel, square, top, bottom = square_group(
            table, place, row_panel, chunks[: h + 1], spans, h, widths, shape
        )
        panels.append(panel)
        squares.append(square)
        strips.append([(top, bottom), *exchange(top, bottom)])

    lo = ROW_GROUP * sum(widths[:-1]) * TILE
    cube = cube_part(strips[:-1], panels, 0, widths)
    return cube_part(strips[-1:], panels, lo, widths, cube, (place, pattern_square, pattern_cube, squares))


def local(density, pattern_p, pattern_square, pattern_cube):
    tile_rows, tile_cols = density.shape[0] // TILE, density.shape[1] // TILE
    if lax.axis_size("row") != ROW_GROUP or tile_cols != sum(WIDTHS):
        return dense_step(density, pattern_p, pattern_square, pattern_cube)
    bounds = chunk_bounds(tile_rows, WIDTHS)
    table = slot_table(pattern_p, tile_rows, tile_cols)
    limit = np.tile(np.repeat(bounds, WIDTHS), table.shape[1] // tile_cols)
    fits = jnp.all(table < jnp.asarray(limit, jnp.int32)[None, :])
    place = jnp.stack([lax.axis_index("col"), lax.axis_index("row")]).astype(jnp.int32)
    spans = list(zip([0, *bounds[:-1]], bounds))
    cut = bounds[-1] // 2
    packed = pack(table, place, density, [(0, cut), (cut, bounds[-1]), spans[0]])
    return lax.cond(
        fits,
        lambda: packed_step(density, table, place, pattern_square, pattern_cube, packed, spans, WIDTHS),
        lambda: dense_step(density, pattern_p, pattern_square, pattern_cube),
    )


def solution(mesh):
    placed = (P("col", "row"), P(), P(), P())
    return jax.shard_map(
        local, mesh=mesh, in_specs=placed, out_specs=P("col", "row"), check_vma=False
    )
```

```python
import functools
import math

import jax
import jax.numpy as jnp
import numpy as np
from jax import lax
from jax.experimental import pallas as pl
from jax.experimental.pallas import tpu as pltpu
from jax.sharding import PartitionSpec as P

TILE = 128
ROW_GROUP = 4
WIDTHS = (4, 4, 4, 4)
SIGMAS = ((3.2, 2.1), (4.2, 3.9))
DEPTH = 1024
VMEM_BYTES = 60 * 2**20
SMEM = pl.BlockSpec(memory_space=pltpu.SMEM)
VMEM = pl.BlockSpec(memory_space=pltpu.VMEM)
ANY = pl.BlockSpec(memory_space=pl.ANY)


def tile_mask(pattern, row_start, col_start, nrows, ncols):
    tile_rows = nrows // TILE + 2
    tile_cols = ncols // TILE + 2
    padded = jnp.pad(pattern, ((0, tile_rows), (0, tile_cols)))
    block = lax.dynamic_slice(
        padded, (row_start // TILE, col_start // TILE), (tile_rows, tile_cols)
    )
    spread = jnp.repeat(jnp.repeat(block, TILE, 0), TILE, 1)
    return lax.dynamic_slice(spread, (row_start % TILE, col_start % TILE), (nrows, ncols))


def dense_step(density, pattern_p, pattern_square, pattern_cube):
    nrows, ncols = density.shape
    row_start = lax.axis_index("col") * nrows
    col_start = lax.axis_index("row") * ncols
    masked = density * tile_mask(pattern_p, row_start, col_start, nrows, ncols).astype(jnp.bfloat16)
    column_panel = lax.all_gather(masked, "col", axis=0, tiled=True)

    def right_fold(piece):
        return jnp.dot(piece, column_panel, preferred_element_type=jnp.float32)

    square = right_fold(lax.all_gather(masked, "row", axis=1, tiled=True))
    cube = right_fold(lax.all_gather(square.astype(jnp.bfloat16), "row", axis=1, tiled=True))
    keep_square = tile_mask(pattern_square, row_start, col_start, nrows, ncols).astype(jnp.float32)
    keep_cube = tile_mask(pattern_cube, row_start, col_start, nrows, ncols).astype(jnp.float32)
    return 3.0 * keep_square * square - 2.0 * keep_cube * cube


def chunk_bounds(tile_rows, widths, part_sigmas, sigmas):
    bounds, cols = [], 0
    for width in widths:
        cols += width
        tiles = tile_rows * cols
        more = (sigmas if cols == sum(widths) else part_sigmas) * math.sqrt(tiles)
        bounds.append(min(tiles, 2 * math.ceil((tiles + more) / 4)))
    return [min(b, bounds[-1]) for b in bounds]


def slot_table(pattern, tile_rows, tile_cols):
    n = pattern.shape[0]
    at = np.arange(n)
    same_rows = at[:, None] // tile_rows == at[None, :] // tile_rows
    above = (same_rows & (at[None, :] < at[:, None])).astype(np.float32)
    same_cols = at[:, None] // tile_cols == at[None, :] // tile_cols
    left = (same_cols & (at[:, None] < at[None, :])).astype(np.float32)
    kept = pattern.astype(jnp.bfloat16)
    dot = functools.partial(jnp.dot, preferred_element_type=jnp.float32)
    in_column = dot(jnp.asarray(above, jnp.bfloat16), kept)
    column = dot(jnp.asarray(same_rows, jnp.bfloat16), kept).astype(jnp.bfloat16)
    before = dot(column, jnp.asarray(left, jnp.bfloat16))
    return jnp.where(pattern != 0, (in_column + before).astype(jnp.int32), -1)


def column_lists(table, place, tile_rows, tile_cols):
    n = table.shape[0]
    blocks = n // tile_rows
    tiles = tile_rows * tile_cols
    mine = lax.dynamic_slice(table, (0, place[1] * tile_cols), (n, tile_cols)).reshape(blocks, tile_rows, tile_cols)
    order = mine.transpose(0, 2, 1).reshape(blocks, tiles, 1)
    which = lax.broadcasted_iota(jnp.int32, (blocks, tiles, tiles), 1)
    slot = lax.broadcasted_iota(jnp.int32, (blocks, tiles, tiles), 2)
    lists = jnp.sum(jnp.where(order == slot, which, 0), 1)
    column = lax.broadcasted_iota(jnp.int32, (blocks, tiles, tile_cols + 1), 1) // tile_rows
    limit = lax.broadcasted_iota(jnp.int32, (blocks, tiles, tile_cols + 1), 2)
    counts = jnp.sum(jnp.where((order >= 0) & (column < limit), 1, 0), 1)
    return lists, counts


def tile_at(ref, i, j):
    return ref.at[pl.ds(pl.multiple_of(i * TILE, TILE), TILE), pl.ds(pl.multiple_of(j * TILE, TILE), TILE)]


def send_kept(table_ref, place_ref, x_ref, outs, sems, spans, shape):
    tile_rows, tile_cols = shape
    c, r = place_ref[0], place_ref[1]

    def send(i, j, slot):
        for q, (lo, hi) in enumerate(spans):
            @pl.when((slot >= lo) & (slot < hi))
            def _():
                pltpu.make_async_copy(tile_at(x_ref, i, j), outs[q].at[slot - lo], sems.at[q]).start()

    def step(n, used):
        j, i = n // tile_rows, n % tile_rows
        slot = table_ref[c * tile_rows + i, r * tile_cols + j]
        send(i, j, slot)
        return used + (slot >= 0).astype(jnp.int32)

    used = lax.fori_loop(0, tile_rows * tile_cols, step, jnp.int32(0))
    top = max(hi for _, hi in spans)

    def fill(slot, z):
        send(0, 0, slot)
        return z

    lax.fori_loop(used, jnp.int32(top), fill, 0)
    for q, out in enumerate(outs):
        pltpu.make_async_copy(out, out, sems.at[q]).wait()


def pack(table, place, density, spans):
    shape = density.shape[0] // TILE, density.shape[1] // TILE

    def kernel(table_ref, place_ref, x_ref, *refs):
        send_kept(table_ref, place_ref, x_ref, refs[:-1], refs[-1], spans, shape)

    return pl.pallas_call(
        kernel,
        out_shape=[jax.ShapeDtypeStruct((hi - lo, TILE, TILE), density.dtype) for lo, hi in spans],
        in_specs=[SMEM, SMEM, VMEM],
        out_specs=[ANY] * len(spans),
        scratch_shapes=[pltpu.SemaphoreType.DMA((len(spans),))],
        name="pack",
    )(table, place, density)


def stage(halves, lo, hi, after):
    cut = halves[0].shape[0]
    parts = []
    if lo < cut:
        parts.append((0, lo, min(hi, cut)))
    if hi > cut:
        parts.append((1, max(lo, cut) - cut, hi - cut))

    def kernel(h0, h1, *refs):
        out, sem = refs[-2:]
        at, copies = 0, []
        for which, first, end in parts:
            src = (h0, h1)[which].at[pl.ds(first, end - first)]
            copies.append(pltpu.make_async_copy(src, out.at[pl.ds(at, end - first)], sem.at[which]))
            at += end - first
        for copy in copies:
            copy.start()
        for copy in copies:
            copy.wait()

    return pl.pallas_call(
        kernel,
        out_shape=jax.ShapeDtypeStruct((hi - lo, TILE, TILE), halves[0].dtype),
        in_specs=[ANY] * (2 + len(after)),
        out_specs=VMEM,
        scratch_shapes=[pltpu.SemaphoreType.DMA((2,))],
        name="stage",
    )(*halves, *after)


def split(x, y, after):
    nrows, ncols = x.shape
    half = jax.ShapeDtypeStruct((nrows // 2, ncols), x.dtype)

    def kernel(x_ref, y_ref, *refs):
        top, bottom, sem = refs[-3:]
        copies = [
            pltpu.make_async_copy(x_ref.at[pl.ds(0, nrows // 2)], top, sem.at[0]),
            pltpu.make_async_copy(y_ref.at[pl.ds(nrows // 2, nrows // 2)], bottom, sem.at[1]),
        ]
        for copy in copies:
            copy.start()
        for copy in copies:
            copy.wait()

    return pl.pallas_call(
        kernel,
        out_shape=[half, half],
        in_specs=[ANY] * (2 + len(after)),
        out_specs=[VMEM, VMEM],
        scratch_shapes=[pltpu.SemaphoreType.DMA((2,))],
        name="split",
    )(x, y, *after)


def row_unpack(table, place, density, pieces, ks, after=()):
    nrows, ncols = density.shape
    tile_rows, tile_cols = nrows // TILE, ncols // TILE
    flat = [x for piece in pieces if piece is not None for x in piece]
    sizes = [x.shape[0] for x in flat[:2]]

    def kernel(table_ref, place_ref, x_ref, *refs):
        ins, (out, held, sems) = refs[: len(flat)], refs[-3:]
        i = pl.program_id(0)
        c, r = place_ref[0], place_ref[1]

        @pl.when(i == 0)
        def _():
            copies = []
            for n, ref in enumerate(ins):
                which = n % 2
                target = held.at[n // 2, pl.ds(which * sizes[0], sizes[which])]
                copies.append(pltpu.make_async_copy(ref, target, sems.at[n]))
            for copy in copies:
                copy.start()
            for copy in copies:
                copy.wait()

        at = 0
        for n, (k, piece) in enumerate(zip(ks, pieces)):
            for j in range(tile_cols):
                slot = table_ref[c * tile_rows + i, (r ^ k) * tile_cols + j]
                if piece is None:
                    tile = x_ref[:, j * TILE : (j + 1) * TILE]
                else:
                    tile = held[at, jnp.maximum(slot, 0)]
                d = n * tile_cols + j
                out[:, d * TILE : (d + 1) * TILE] = jnp.where(slot >= 0, tile, jnp.zeros_like(tile))
            at += piece is not None

    return pl.pallas_call(
        kernel,
        grid=(tile_rows,),
        out_shape=jax.ShapeDtypeStruct((nrows, len(ks) * ncols), jnp.bfloat16),
        in_specs=[SMEM, SMEM, pl.BlockSpec((TILE, ncols), lambda i: (i, 0))] + [ANY] * (len(flat) + len(after)),
        out_specs=pl.BlockSpec((TILE, len(ks) * ncols), lambda i: (i, 0)),
        scratch_shapes=[
            pltpu.VMEM((len(flat) // 2, sum(sizes), TILE, TILE), jnp.bfloat16),
            pltpu.SemaphoreType.DMA((len(flat),)),
        ],
        compiler_params=pltpu.CompilerParams(vmem_limit_bytes=VMEM_BYTES),
        cost_estimate=pl.CostEstimate(flops=0, bytes_accessed=8 * len(ks) * nrows * ncols, transcendentals=0),
        name="row_unpack",
    )(table, place, density, *flat, *after)


def square_group(lists, counts, place, row_parts, chunks, spans, first, width, shape, ks, partial=None, after=()):
    tile_rows, tile_cols = shape
    nrows = row_parts[0].shape[0]
    span = tile_cols * TILE
    count = len(ks)
    depth = count * span
    n = width * TILE
    bits = (tile_cols * width).bit_length()
    step_rows = nrows // 2

    def kernel(lists_ref, counts_ref, place_ref, *refs):
        a_refs, refs = refs[: len(row_parts)], refs[len(row_parts) :]
        ins, refs = refs[: len(chunks)], refs[len(chunks) :]
        if partial is not None:
            partial_ref, refs = refs[0], refs[1:]
        panel_out, square, low, a, panel, kept, a_sems, sems, out_sem, partial_sem = refs[len(after) :]
        r = place_ref[1]
        owners = tile_cols // tile_rows

        part = at = 0
        for k in range(count):
            source = a_refs[part].at[:, pl.ds(at, span)]
            pltpu.make_async_copy(source, a.at[k], a_sems.at[k]).start()
            at += span
            if at == row_parts[part].shape[1]:
                part, at = part + 1, 0
        if partial is not None:
            before = pltpu.make_async_copy(partial_ref, square, partial_sem)
            before.start()

        def fetch(k, z):
            rows = pl.ds(pl.multiple_of(k * span, span), span)
            panel[:, rows] = jnp.zeros((width, span, TILE), panel.dtype)
            total = jnp.int32(0)
            for o in range(owners):
                owner = (r ^ (k + ks[0])) * owners + o
                begin, end = counts_ref[owner, first], counts_ref[owner, first + width]
                total += end - begin
                top = k * span + o * tile_rows * TILE
                for q, (lo, hi) in enumerate(spans[: len(chunks)]):
                    shift = owner * (hi - lo) - lo

                    def one(slot, z):
                        tile = lists_ref[owner, slot]
                        j, i = tile // tile_rows - first, tile % tile_rows
                        here = pl.ds(pl.multiple_of(top + i * TILE, TILE), TILE)
                        pltpu.make_async_copy(ins[q].at[shift + slot], panel.at[j, here], sems.at[k]).start()
                        return z

                    lax.fori_loop(jnp.maximum(begin, lo), jnp.minimum(end, hi), one, 0)
            kept[k] = total
            return z

        lax.fori_loop(0, count, fetch, 0)

        def out_copy(k):
            rows = pl.ds(pl.multiple_of(k * span, span), span)
            return pltpu.make_async_copy(panel.at[:, rows], panel_out.at[:, rows], out_sem)

        def multiply(k, z):
            for bit in range(bits):
                some = ins[0].at[pl.ds(0, 1 << bit)]

                @pl.when((kept[k] >> bit) & 1 == 1)
                def _():
                    pltpu.make_async_copy(some, some, sems.at[k]).wait()

            pltpu.make_async_copy(a.at[k], a.at[k], a_sems.at[k]).wait()
            out_copy(k).start()
            rows = pl.ds(pl.multiple_of(k * span, span), span)

            def step(m, z):
                here = pl.ds(pl.multiple_of(m * step_rows, step_rows), step_rows)
                right = jnp.concatenate([panel[j, rows] for j in range(width)], 1)
                square[here] += jnp.dot(a[k, here], right, preferred_element_type=jnp.float32)
                return z

            return lax.fori_loop(0, nrows // step_rows, step, z)

        if partial is not None:
            before.wait()
        else:
            square[...] = jnp.zeros_like(square)
        lax.fori_loop(0, count, multiply, 0)
        low[...] = square[...].astype(jnp.bfloat16)
        for k in range(count):
            out_copy(k).wait()

    operands = [*row_parts, *chunks, *([] if partial is None else [partial]), *after]
    return pl.pallas_call(
        kernel,
        out_shape=[
            jax.ShapeDtypeStruct((width, depth, TILE), jnp.bfloat16),
            jax.ShapeDtypeStruct((nrows, n), jnp.float32),
            jax.ShapeDtypeStruct((nrows, n), jnp.bfloat16),
        ],
        in_specs=[SMEM] * 3 + [ANY] * len(operands),
        out_specs=[ANY, VMEM, VMEM],
        scratch_shapes=[
            pltpu.VMEM((count, nrows, span), jnp.bfloat16),
            pltpu.VMEM((width, depth, TILE), jnp.bfloat16),
            pltpu.SMEM((count,), jnp.int32),
            pltpu.SemaphoreType.DMA((count,)),
            pltpu.SemaphoreType.DMA((count,)),
            pltpu.SemaphoreType.DMA,
            pltpu.SemaphoreType.DMA,
        ],
        compiler_params=pltpu.CompilerParams(vmem_limit_bytes=VMEM_BYTES),
        cost_estimate=pl.CostEstimate(
            flops=2 * nrows * depth * n, bytes_accessed=2 * depth * (nrows + 2 * n) + 6 * nrows * n, transcendentals=0
        ),
        name="square_group",
    )(lists, counts, place, *operands)


def cube_part(strips, panels, jobs, widths, before, finish=None, after=()):
    groups = sorted({g for job in jobs.values() for g in job})
    firsts = [sum(widths[:h]) for h in range(len(widths))]
    span = sum(widths) * TILE
    nrows = strips[groups[0]][0][0][0].shape[0]
    lefts, start = [], {}
    at = 0
    for g in groups:
        start[g] = at
        for pieces in strips[g]:
            lefts += [(x, row, at) for x, row in pieces]
            at += widths[g] * TILE
    total = at
    hs = list(jobs)
    deepest = max(ROW_GROUP * TILE * sum(widths[g] for g in job) for job in jobs.values())
    widest = max(widths[h] for h in hs)
    panel_arrays = [x for h in hs for x, _ in panels[h]]
    operands = [x for x, *_ in lefts] + panel_arrays + [before[h] for h in hs if h in before]
    with_before = [h for h in hs if h in before]
    specs = [ANY] * len(operands)
    if finish is not None:
        place, pattern_square, pattern_cube, squares = finish
        operands += [place, pattern_square, pattern_cube, *squares]
        specs += [SMEM] * 3 + [ANY] * len(squares)
        out_shape = [jax.ShapeDtypeStruct((nrows, span), jnp.float32)]
    else:
        out_shape = [jax.ShapeDtypeStruct((nrows, widths[h] * TILE), jnp.float32) for h in hs]
    operands += after
    specs += [ANY] * len(after)
    step_rows = nrows // 2

    def kernel(*refs):
        refs = list(refs)

        def take(count):
            taken = refs[:count]
            del refs[:count]
            return taken

        left_refs = take(len(lefts))
        panel_refs = {h: take(ROW_GROUP) for h in hs}
        before_refs = dict(zip(with_before, take(len(with_before))))
        if finish is not None:
            place_ref, keep_square, keep_cube = take(3)
            square_refs = take(len(hs))
        take(len(after))
        outs = take(len(out_shape))
        left, right, acc, held, left_sems, right_sems, acc_sems, held_sems, out_sems = refs

        def loads(n):
            h, s, t = hs[n], n % 2, n % 3
            lanes = pl.ds(0, widths[h] * TILE)
            copies, at = [], 0
            for g in jobs[h]:
                rows = widths[g] * TILE
                for k, (ref, (_, shift)) in enumerate(zip(panel_refs[h], panels[h])):
                    source = ref.at[:, pl.ds(shift + firsts[g] * TILE, rows)]
                    target = right.at[s, pl.ds(0, widths[h]), pl.ds(at, rows)]
                    copies.append(pltpu.make_async_copy(source, target, right_sems.at[s]))
                    at += rows
            if h in before_refs:
                copies.append(pltpu.make_async_copy(before_refs[h], acc.at[t, :, lanes], acc_sems.at[t]))
            if finish is not None:
                copies.append(pltpu.make_async_copy(square_refs[n], held.at[t, :, lanes], held_sems.at[t]))
            return copies

        def store(n):
            h, t = hs[n], n % 3
            lanes = pl.ds(0, widths[h] * TILE)
            if finish is None:
                return pltpu.make_async_copy(acc.at[t, :, lanes], outs[n], out_sems.at[t])
            target = outs[0].at[:, pl.ds(firsts[h] * TILE, widths[h] * TILE)]
            return pltpu.make_async_copy(held.at[t, :, lanes], target, out_sems.at[t])

        left_copies = [
            pltpu.make_async_copy(ref, left.at[pl.ds(row, x.shape[0]), pl.ds(col, x.shape[1])], left_sems.at[0])
            for ref, (x, row, col) in zip(left_refs, lefts)
        ]
        for copy in left_copies + loads(0):
            copy.start()
        for copy in left_copies:
            copy.wait()
        for n, h in enumerate(hs):
            s, t, wide = n % 2, n % 3, widths[h] * TILE
            if n >= 2:
                store(n - 2).wait()
            if n + 1 < len(hs):
                for copy in loads(n + 1):
                    copy.start()
            for copy in loads(n):
                copy.wait()
            if h not in before_refs:
                acc[t, :, :wide] = jnp.zeros((nrows, wide), jnp.float32)
            shift = start[jobs[h][0]]
            blocks = ROW_GROUP * TILE * sum(widths[g] for g in jobs[h]) // DEPTH

            def step(b, z):
                here = pl.ds(pl.multiple_of(b * DEPTH, DEPTH), DEPTH)
                there = pl.ds(pl.multiple_of(shift + b * DEPTH, DEPTH), DEPTH)

                def rows_step(m, z):
                    rows = pl.ds(pl.multiple_of(m * step_rows, step_rows), step_rows)
                    other = jnp.concatenate([right[s, j, here] for j in range(widths[h])], 1)
                    part = jnp.dot(left[rows, there], other, preferred_element_type=jnp.float32)
                    acc[t, rows, :wide] += part
                    return z

                return lax.fori_loop(0, nrows // step_rows, rows_step, z)

            lax.fori_loop(0, blocks, step, 0)
            if finish is not None:
                tile_rows, tile_cols = nrows // TILE, span // TILE
                row, col = place_ref[0] * tile_rows, place_ref[1] * tile_cols + firsts[h]

                def combine(i, z):
                    rows = pl.ds(pl.multiple_of(i * TILE, TILE), TILE)
                    for j in range(widths[h]):
                        lanes = slice(j * TILE, (j + 1) * TILE)
                        a = 3.0 * keep_square[row + i, col + j].astype(jnp.float32)
                        b = 2.0 * keep_cube[row + i, col + j].astype(jnp.float32)
                        held[t, rows, lanes] = a * held[t, rows, lanes] - b * acc[t, rows, lanes]
                    return z

                lax.fori_loop(0, tile_rows, combine, 0)
            store(n).start()
        for n in range(max(len(hs) - 2, 0), len(hs)):
            store(n).wait()

    flops = sum(2 * nrows * ROW_GROUP * TILE * widths[g] * widths[h] * TILE for h in hs for g in jobs[h])
    return pl.pallas_call(
        kernel,
        out_shape=out_shape,
        in_specs=specs,
        out_specs=[ANY] * len(out_shape),
        scratch_shapes=[
            pltpu.VMEM((nrows, total), jnp.bfloat16),
            pltpu.VMEM((2, widest, deepest, TILE), jnp.bfloat16),
            pltpu.VMEM((3, nrows, widest * TILE), jnp.float32),
            pltpu.VMEM((3, nrows, widest * TILE) if finish is not None else (3, 8, TILE), jnp.float32),
            pltpu.SemaphoreType.DMA((1,)),
            pltpu.SemaphoreType.DMA((2,)),
            pltpu.SemaphoreType.DMA((3,)),
            pltpu.SemaphoreType.DMA((3,)),
            pltpu.SemaphoreType.DMA((3,)),
        ],
        compiler_params=pltpu.CompilerParams(vmem_limit_bytes=VMEM_BYTES),
        cost_estimate=pl.CostEstimate(flops=flops, bytes_accessed=8 * nrows * span, transcendentals=0),
        name="cube_part",
    )(*operands)


def packed_step(density, table, place, pattern_square, pattern_cube, spans):
    nrows, ncols = density.shape
    shape = nrows // TILE, ncols // TILE
    widths = WIDTHS
    cap = spans[-1][1]
    *halves, first_chunk = pack(table, place, density, [(0, cap // 2), (cap // 2, cap), spans[0]])

    def swap(x, k):
        return lax.ppermute(x, "row", [(i, i ^ k) for i in range(ROW_GROUP)])

    def gather(x):
        return lax.all_gather(x, "col", axis=0, tiled=True)

    chunks = [gather(first_chunk)]
    by_x, by_y = [swap(x, 1) for x in halves], [swap(x, 2) for x in halves]
    chunks.append(gather(stage(halves, *spans[1], by_x + by_y)))
    far = [swap(by_x[0], 2), swap(by_y[1], 1)]
    near_part = row_unpack(table, place, density, [None, by_x, by_y], [0, 1, 2])

    lists, counts = column_lists(table, place, *shape)
    group = functools.partial(square_group, lists, counts, place)
    panels, squares, strips = [], [], []

    def send(square, low):
        squares.append(square)
        strips.append([[(low, 0)], [(swap(low, 1), 0)], [(swap(low, 2), 0)]])

    def forward(h, after=()):
        (x, _), (y, _) = strips[h][1][0], strips[h][2][0]
        top, bottom = split(x, y, after)
        strips[h].append([(swap(top, 2), 0), (swap(bottom, 1), nrows // 2)])
        return top

    near_panel, partial, _ = group([near_part], chunks[:1], spans, 0, widths[0], shape, [0, 1, 2])
    far_part = row_unpack(table, place, density, [far], [3], [partial])
    chunks.append(gather(stage(halves, *spans[2], [far_part])))
    far_panel, square, low = group([far_part], chunks[:1], spans, 0, widths[0], shape, [3], partial)
    panels.append([(near_panel, k * ncols) for k in range(3)] + [(far_panel, 0)])
    send(square, low)

    def next_group(h, after):
        parts = [near_part, far_part]
        panel, square, low = group(
            parts, chunks[: h + 1], spans, sum(widths[:h]), widths[h], shape, [0, 1, 2, 3], None, after
        )
        panels.append([(panel, k * ncols) for k in range(ROW_GROUP)])
        send(square, low)

    next_group(1, [])
    forward(0)
    chunks.append(gather(stage(halves, *spans[3], [low])))
    next_group(2, [forward(1)])
    cubes = dict(enumerate(cube_part(strips, panels, {0: [0, 1], 1: [0, 1]}, widths, {}, after=[squares[2]])))
    next_group(3, [forward(2), cubes[0]])
    jobs = {0: [2], 1: [2], 2: [0, 1, 2], 3: [0, 1, 2]}
    cubes = dict(enumerate(cube_part(strips, panels, jobs, widths, cubes)))
    forward(3, [cubes[0]])
    finish = place, pattern_square, pattern_cube, squares
    return cube_part(strips, panels, {h: [3] for h in range(4)}, widths, cubes, finish)[0]


def local(density, pattern_p, pattern_square, pattern_cube):
    tile_rows, tile_cols = density.shape[0] // TILE, density.shape[1] // TILE
    if lax.axis_size("row") != ROW_GROUP or tile_cols != sum(WIDTHS):
        return dense_step(density, pattern_p, pattern_square, pattern_cube)
    widths = WIDTHS
    table = slot_table(pattern_p, tile_rows, tile_cols)
    place = jnp.stack([lax.axis_index("col"), lax.axis_index("row")]).astype(jnp.int32)
    level, ways = len(SIGMAS), []
    for n, sigmas in reversed(list(enumerate(SIGMAS))):
        bounds = chunk_bounds(tile_rows, widths, *sigmas)
        limit = np.tile(np.repeat(bounds, widths), table.shape[1] // tile_cols)
        fits = jnp.all(table < jnp.asarray(limit, jnp.int32)[None, :])
        level = jnp.where(fits, n, level)
        spans = list(zip([0, *bounds[:-1]], bounds))
        ways.insert(0, functools.partial(
            packed_step, density, table, place, pattern_square, pattern_cube, spans
        ))
    ways.append(lambda: dense_step(density, pattern_p, pattern_square, pattern_cube))
    return lax.switch(level, ways)


def solution(mesh):
    placed = (P("col", "row"), P(), P(), P())
    return jax.shard_map(
        local, mesh=mesh, in_specs=placed, out_specs=P("col", "row"), check_vma=False
    )
```

```python
import functools
import math

import jax
import jax.numpy as jnp
import numpy as np
from jax import lax
from jax.experimental import pallas as pl
from jax.experimental.pallas import tpu as pltpu
from jax.sharding import PartitionSpec as P

TILE = 128
ROW_GROUP = 4
WIDTHS = (4, 4, 4, 4)
SIGMAS = ((3.2, 2.1), (4.2, 3.5))
SMALL = pl.CostEstimate(flops=1, bytes_accessed=1, transcendentals=0)
VMEM_BYTES = 60 * 2**20
SMEM = pl.BlockSpec(memory_space=pltpu.SMEM)
VMEM = pl.BlockSpec(memory_space=pltpu.VMEM)
ANY = pl.BlockSpec(memory_space=pl.ANY)


def tile_mask(pattern, row_start, col_start, nrows, ncols):
    tile_rows = nrows // TILE + 2
    tile_cols = ncols // TILE + 2
    padded = jnp.pad(pattern, ((0, tile_rows), (0, tile_cols)))
    block = lax.dynamic_slice(
        padded, (row_start // TILE, col_start // TILE), (tile_rows, tile_cols)
    )
    spread = jnp.repeat(jnp.repeat(block, TILE, 0), TILE, 1)
    return lax.dynamic_slice(spread, (row_start % TILE, col_start % TILE), (nrows, ncols))


def dense_step(density, pattern_p, pattern_square, pattern_cube):
    nrows, ncols = density.shape
    row_start = lax.axis_index("col") * nrows
    col_start = lax.axis_index("row") * ncols
    masked = density * tile_mask(pattern_p, row_start, col_start, nrows, ncols).astype(jnp.bfloat16)
    column_panel = lax.all_gather(masked, "col", axis=0, tiled=True)

    def right_fold(piece):
        return jnp.dot(piece, column_panel, preferred_element_type=jnp.float32)

    square = right_fold(lax.all_gather(masked, "row", axis=1, tiled=True))
    cube = right_fold(lax.all_gather(square.astype(jnp.bfloat16), "row", axis=1, tiled=True))
    keep_square = tile_mask(pattern_square, row_start, col_start, nrows, ncols).astype(jnp.float32)
    keep_cube = tile_mask(pattern_cube, row_start, col_start, nrows, ncols).astype(jnp.float32)
    return 3.0 * keep_square * square - 2.0 * keep_cube * cube


def chunk_bounds(tile_rows, widths, part_sigmas, sigmas):
    bounds, cols = [], 0
    for width in widths:
        cols += width
        tiles = tile_rows * cols
        more = (sigmas if cols == sum(widths) else part_sigmas) * math.sqrt(tiles)
        bounds.append(min(tiles, 2 * math.ceil((tiles + more) / 4)))
    return [min(b, bounds[-1]) for b in bounds]


def slot_table(pattern, tile_rows, tile_cols):
    n = pattern.shape[0]
    at = np.arange(n)
    same_rows = at[:, None] // tile_rows == at[None, :] // tile_rows
    above = (same_rows & (at[None, :] < at[:, None])).astype(np.float32)
    same_cols = at[:, None] // tile_cols == at[None, :] // tile_cols
    left = (same_cols & (at[:, None] < at[None, :])).astype(np.float32)
    kept = pattern.astype(jnp.bfloat16)
    dot = functools.partial(jnp.dot, preferred_element_type=jnp.float32)
    in_column = dot(jnp.asarray(above, jnp.bfloat16), kept)
    column = dot(jnp.asarray(same_rows, jnp.bfloat16), kept).astype(jnp.bfloat16)
    before = dot(column, jnp.asarray(left, jnp.bfloat16))
    return jnp.where(pattern != 0, (in_column + before).astype(jnp.int32), -1)


def column_lists(table, place, tile_rows, tile_cols):
    n = table.shape[0]
    blocks = n // tile_rows
    tiles = tile_rows * tile_cols
    mine = lax.dynamic_slice(table, (0, place[1] * tile_cols), (n, tile_cols)).reshape(blocks, tile_rows, tile_cols)
    order = mine.transpose(0, 2, 1).reshape(blocks, tiles, 1)
    which = lax.broadcasted_iota(jnp.int32, (blocks, tiles, tiles), 1)
    slot = lax.broadcasted_iota(jnp.int32, (blocks, tiles, tiles), 2)
    spot = which // tile_rows * n + which % tile_rows
    lists = jnp.sum(jnp.where(order == slot, spot, 0), 1)
    column = lax.broadcasted_iota(jnp.int32, (blocks, tiles, tile_cols + 1), 1) // tile_rows
    limit = lax.broadcasted_iota(jnp.int32, (blocks, tiles, tile_cols + 1), 2)
    counts = jnp.sum(jnp.where((order >= 0) & (column < limit), 1, 0), 1)
    return lists, counts


def tile_at(ref, i, j):
    return ref.at[pl.ds(pl.multiple_of(i * TILE, TILE), TILE), pl.ds(pl.multiple_of(j * TILE, TILE), TILE)]


def send_kept(table_ref, place_ref, x_ref, outs, sems, spans, shape):
    tile_rows, tile_cols = shape
    c, r = place_ref[0], place_ref[1]

    def send(i, j, slot):
        for q, (lo, hi) in enumerate(spans):
            @pl.when((slot >= lo) & (slot < hi))
            def _():
                pltpu.make_async_copy(tile_at(x_ref, i, j), outs[q].at[slot - lo], sems.at[q]).start()

    def step(n, used):
        j, i = n // tile_rows, n % tile_rows
        slot = table_ref[c * tile_rows + i, r * tile_cols + j]
        send(i, j, slot)
        return used + (slot >= 0).astype(jnp.int32)

    used = lax.fori_loop(0, tile_rows * tile_cols, step, jnp.int32(0))
    top = max(hi for _, hi in spans)

    def fill(slot, z):
        send(0, 0, slot)
        return z

    lax.fori_loop(used, jnp.int32(top), fill, 0)
    for q, out in enumerate(outs):
        pltpu.make_async_copy(out, out, sems.at[q]).wait()


def pack(table, place, density, spans):
    shape = density.shape[0] // TILE, density.shape[1] // TILE

    def kernel(table_ref, place_ref, x_ref, *refs):
        send_kept(table_ref, place_ref, x_ref, refs[:-1], refs[-1], spans, shape)

    return pl.pallas_call(
        kernel,
        out_shape=[jax.ShapeDtypeStruct((hi - lo, TILE, TILE), density.dtype) for lo, hi in spans],
        in_specs=[SMEM, SMEM, VMEM],
        out_specs=[ANY] * len(spans),
        scratch_shapes=[pltpu.SemaphoreType.DMA((len(spans),))],
        name="pack",
    )(table, place, density)


def stage(halves, lo, hi, after):
    cut = halves[0].shape[0]
    parts = []
    if lo < cut:
        parts.append((0, lo, min(hi, cut)))
    if hi > cut:
        parts.append((1, max(lo, cut) - cut, hi - cut))

    def kernel(h0, h1, *refs):
        out, sem = refs[-2:]
        at, copies = 0, []
        for which, first, end in parts:
            src = (h0, h1)[which].at[pl.ds(first, end - first)]
            copies.append(pltpu.make_async_copy(src, out.at[pl.ds(at, end - first)], sem.at[which]))
            at += end - first
        for copy in copies:
            copy.start()
        for copy in copies:
            copy.wait()

    return pl.pallas_call(
        kernel,
        out_shape=jax.ShapeDtypeStruct((hi - lo, TILE, TILE), halves[0].dtype),
        in_specs=[ANY] * (2 + len(after)),
        out_specs=VMEM,
        scratch_shapes=[pltpu.SemaphoreType.DMA((2,))],
        name="stage",
    )(*halves, *after)


def split(x, y, after):
    nrows, ncols = x.shape
    half = jax.ShapeDtypeStruct((nrows // 2, ncols), x.dtype)

    def kernel(x_ref, y_ref, *refs):
        top, bottom, sem = refs[-3:]
        copies = [
            pltpu.make_async_copy(x_ref.at[pl.ds(0, nrows // 2)], top, sem.at[0]),
            pltpu.make_async_copy(y_ref.at[pl.ds(nrows // 2, nrows // 2)], bottom, sem.at[1]),
        ]
        for copy in copies:
            copy.start()
        for copy in copies:
            copy.wait()

    return pl.pallas_call(
        kernel,
        out_shape=[half, half],
        in_specs=[ANY] * (2 + len(after)),
        out_specs=[VMEM, VMEM],
        scratch_shapes=[pltpu.SemaphoreType.DMA((2,))],
        name="split",
    )(x, y, *after)


def row_unpack(table, place, density, pieces, ks, after=()):
    nrows, ncols = density.shape
    tile_rows, tile_cols = nrows // TILE, ncols // TILE
    flat = [x for piece in pieces if piece is not None for x in piece]
    sizes = [x.shape[0] for x in flat[:2]]

    def kernel(table_ref, place_ref, x_ref, *refs):
        ins, (out, held, sems) = refs[: len(flat)], refs[-3:]
        i = pl.program_id(0)
        c, r = place_ref[0], place_ref[1]

        @pl.when(i == 0)
        def _():
            copies = []
            for n, ref in enumerate(ins):
                which = n % 2
                target = held.at[n // 2, pl.ds(which * sizes[0], sizes[which])]
                copies.append(pltpu.make_async_copy(ref, target, sems.at[n]))
            for copy in copies:
                copy.start()
            for copy in copies:
                copy.wait()

        at = 0
        for n, (k, piece) in enumerate(zip(ks, pieces)):
            for j in range(tile_cols):
                slot = table_ref[c * tile_rows + i, (r ^ k) * tile_cols + j]
                if piece is None:
                    tile = x_ref[:, j * TILE : (j + 1) * TILE]
                else:
                    tile = held[at, jnp.maximum(slot, 0)]
                d = n * tile_cols + j
                out[:, d * TILE : (d + 1) * TILE] = jnp.where(slot >= 0, tile, jnp.zeros_like(tile))
            at += piece is not None

    return pl.pallas_call(
        kernel,
        grid=(tile_rows,),
        out_shape=jax.ShapeDtypeStruct((nrows, len(ks) * ncols), jnp.bfloat16),
        in_specs=[SMEM, SMEM, pl.BlockSpec((TILE, ncols), lambda i: (i, 0))] + [ANY] * (len(flat) + len(after)),
        out_specs=pl.BlockSpec((TILE, len(ks) * ncols), lambda i: (i, 0)),
        scratch_shapes=[
            pltpu.VMEM((len(flat) // 2, sum(sizes), TILE, TILE), jnp.bfloat16),
            pltpu.SemaphoreType.DMA((len(flat),)),
        ],
        compiler_params=pltpu.CompilerParams(vmem_limit_bytes=VMEM_BYTES),
        cost_estimate=SMALL,
        name="row_unpack",
    )(table, place, density, *flat, *after)


def square_group(lists, counts, place, row_parts, chunks, spans, first, width, shape, ks, partial=None, after=()):
    tile_rows, tile_cols = shape
    nrows = row_parts[0].shape[0]
    span = tile_cols * TILE
    count = len(ks)
    depth = count * span
    n = width * TILE
    n_tiles = ROW_GROUP * tile_cols
    bits = (tile_cols * width).bit_length()

    def kernel(lists_ref, counts_ref, place_ref, *refs):
        a_refs, refs = refs[: len(row_parts)], refs[len(row_parts) :]
        ins, refs = refs[: len(chunks)], refs[len(chunks) :]
        if partial is not None:
            partial_ref, refs = refs[0], refs[1:]
        panel_out, square, low, a, panel, kept, a_sems, sems, out_sem, partial_sem = refs[len(after) :]
        r = place_ref[1]
        owners = tile_cols // tile_rows

        part = at = 0
        for k in range(count):
            source = a_refs[part].at[:, pl.ds(at, span)]
            pltpu.make_async_copy(source, a.at[k], a_sems.at[k]).start()
            at += span
            if at == row_parts[part].shape[1]:
                part, at = part + 1, 0
        if partial is not None:
            before = pltpu.make_async_copy(partial_ref, square, partial_sem)
            before.start()

        def fetch(k, z):
            for j in range(width):
                at = pl.ds(j * n_tiles + k * tile_cols, tile_cols)
                panel[at] = jnp.zeros((tile_cols, TILE, TILE), panel.dtype)
            total = jnp.int32(0)
            for o in range(owners):
                owner = (r ^ (k + ks[0])) * owners + o
                begin, end = counts_ref[owner, first], counts_ref[owner, first + width]
                total += end - begin
                base = k * tile_cols + o * tile_rows - first * n_tiles
                for q, (lo, hi) in enumerate(spans[: len(chunks)]):
                    shift = owner * (hi - lo) - lo

                    def one(slot, z):
                        target = panel.at[base + lists_ref[owner, slot]]
                        pltpu.make_async_copy(ins[q].at[shift + slot], target, sems.at[k]).start()
                        return z

                    lax.fori_loop(jnp.maximum(begin, lo), jnp.minimum(end, hi), one, 0)
            kept[k] = total
            return z

        lax.fori_loop(0, count, fetch, 0)

        def out_copies(k):
            rows = pl.ds(k * tile_cols, tile_cols)
            return [
                pltpu.make_async_copy(panel.at[pl.ds(j * n_tiles + k * tile_cols, tile_cols)], panel_out.at[j, rows], out_sem)
                for j in range(width)
            ]

        def multiply(k, z):
            for bit in range(bits):
                some = ins[0].at[pl.ds(0, 1 << bit)]

                @pl.when((kept[k] >> bit) & 1 == 1)
                def _():
                    pltpu.make_async_copy(some, some, sems.at[k]).wait()

            pltpu.make_async_copy(a.at[k], a.at[k], a_sems.at[k]).wait()
            for copy in out_copies(k):
                copy.start()
            right = jnp.concatenate([
                panel[pl.ds(j * n_tiles + k * tile_cols, tile_cols)].reshape(span, TILE) for j in range(width)
            ], 1)
            square[...] += jnp.dot(a[k], right, preferred_element_type=jnp.float32)
            return z

        if partial is not None:
            before.wait()
        else:
            square[...] = jnp.zeros_like(square)
        lax.fori_loop(0, count, multiply, 0)
        low[...] = square[...].astype(jnp.bfloat16)
        for k in range(count):
            for copy in out_copies(k):
                copy.wait()

    operands = [*row_parts, *chunks, *([] if partial is None else [partial]), *after]
    return pl.pallas_call(
        kernel,
        out_shape=[
            jax.ShapeDtypeStruct((width, count * tile_cols, TILE, TILE), jnp.bfloat16),
            jax.ShapeDtypeStruct((nrows, n), jnp.float32),
            jax.ShapeDtypeStruct((nrows, n), jnp.bfloat16),
        ],
        in_specs=[SMEM] * 3 + [ANY] * len(operands),
        out_specs=[ANY, VMEM, VMEM],
        scratch_shapes=[
            pltpu.VMEM((count, nrows, span), jnp.bfloat16),
            pltpu.VMEM((width * n_tiles, TILE, TILE), jnp.bfloat16),
            pltpu.SMEM((count,), jnp.int32),
            pltpu.SemaphoreType.DMA((count,)),
            pltpu.SemaphoreType.DMA((count,)),
            pltpu.SemaphoreType.DMA,
            pltpu.SemaphoreType.DMA,
        ],
        compiler_params=pltpu.CompilerParams(vmem_limit_bytes=VMEM_BYTES),
        cost_estimate=SMALL,
        name="square_group",
    )(lists, counts, place, *operands)


def cube_part(strips, panels, jobs, widths, before, keep=None, squares=None, base=None, joined=False, after=()):
    groups = sorted({g for job in jobs.values() for g in job})
    firsts = [sum(widths[:h]) for h in range(len(widths))]
    tile_cols = sum(widths)
    span = tile_cols * TILE
    nrows = strips[0][0][0][0].shape[0]
    tile_rows = nrows // TILE
    lefts, start = [], {}
    at = 0
    for group in groups:
        g, ks = group
        start[group] = at
        for k in ks:
            lefts += [(x, row, at, group) for x, row in strips[g][k]]
            at += widths[g] * TILE
    total = at
    hs = list(jobs)
    deepest = max(sum(len(ks) * widths[g] for g, ks in job) for job in jobs.values())
    widest = max(widths[h] for h in hs)
    with_before = [h for h in hs if h in before]
    held_from = base if base is not None else squares
    operands = [x for x, *_ in lefts] + [x for h in hs for x, _ in panels[h]] + [before[h] for h in with_before]
    specs = [ANY] * len(operands)
    if keep is not None:
        operands += [*keep, *(held_from[h] for h in hs)]
        specs += [SMEM] * 3 + [ANY] * len(hs)
    operands += after
    specs += [ANY] * len(after)
    if joined:
        out_shape = [jax.ShapeDtypeStruct((nrows, span), jnp.float32)]
    else:
        out_shape = [jax.ShapeDtypeStruct((nrows, widths[h] * TILE), jnp.float32) for h in hs]

    def kernel(*refs):
        refs = list(refs)

        def take(count):
            taken = refs[:count]
            del refs[:count]
            return taken

        left_refs = take(len(lefts))
        panel_refs = {h: take(ROW_GROUP) for h in hs}
        before_refs = dict(zip(with_before, take(len(with_before))))
        if keep is not None:
            place_ref, keep_square, keep_cube = take(3)
            held_refs = dict(zip(hs, take(len(hs))))
        take(len(after))
        outs = take(len(out_shape))
        left, right, acc, held, left_sems, right_sems, acc_sems, held_sems, out_sems = refs

        def left_copies(g):
            return [
                pltpu.make_async_copy(
                    ref, left.at[pl.ds(row, x.shape[0]), pl.ds(at, x.shape[1])], left_sems.at[groups.index(g)]
                )
                for ref, (x, row, at, group) in zip(left_refs, lefts)
                if group == g
            ]

        def right_copies(n, at, group):
            h, s = hs[n], n % 2
            g, ks = group
            copies = []
            for m, k in enumerate(ks):
                ref, shift = panel_refs[h][k], panels[h][k][1]
                copies.append(pltpu.make_async_copy(
                    ref.at[:, pl.ds(shift + firsts[g], widths[g])],
                    right.at[s, pl.ds(0, widths[h]), pl.ds(at + m * widths[g], widths[g])],
                    right_sems.at[s, jobs[h].index(group)],
                ))
            return copies

        def acc_copies(n):
            h, t = hs[n], n % 3
            lanes = pl.ds(0, widths[h] * TILE)
            copies = []
            if h in before_refs:
                copies.append(pltpu.make_async_copy(before_refs[h], acc.at[t, :, lanes], acc_sems.at[t]))
            return copies

        def held_copies(n):
            h, t = hs[n], n % 3
            lanes = pl.ds(0, widths[h] * TILE)
            copies = []
            if keep is not None:
                copies.append(pltpu.make_async_copy(held_refs[h], held.at[t, :, lanes], held_sems.at[t]))
            return copies

        def steps(h):
            at, found = 0, []
            for g in jobs[h]:
                found.append((at, g))
                at += len(g[1]) * widths[g[0]]
            return found

        def loads(n):
            copies = []
            for m, (at, g) in enumerate(steps(hs[n])):
                if n == 0:
                    copies += left_copies(g)
                copies += right_copies(n, at, g)
                if m == 0:
                    copies += acc_copies(n)
            if n == 0:
                copies += [copy for g in groups if g not in jobs[hs[0]] for copy in left_copies(g)]
            return copies + held_copies(n)

        def store(n):
            h, t = hs[n], n % 3
            lanes = pl.ds(0, widths[h] * TILE)
            source = (acc if keep is None else held).at[t, :, lanes]
            target = outs[n] if not joined else outs[0].at[:, pl.ds(firsts[h] * TILE, widths[h] * TILE)]
            return pltpu.make_async_copy(source, target, out_sems.at[t])

        for copy in loads(0):
            copy.start()
        arrived = set()
        for n, h in enumerate(hs):
            s, t, wide = n % 2, n % 3, widths[h] * TILE
            if n >= 2:
                store(n - 2).wait()
            if n + 1 < len(hs):
                for copy in loads(n + 1):
                    copy.start()
            row, col = (place_ref[0] * tile_rows, place_ref[1] * tile_cols + firsts[h]) if keep is not None else (0, 0)
            for copy in acc_copies(n):
                copy.wait()
            found = steps(h)
            for m, (at, g) in enumerate(found):
                if g not in arrived:
                    arrived.add(g)
                    for copy in left_copies(g):
                        copy.wait()
                for copy in right_copies(n, at, g):
                    copy.wait()
                last = m == len(found) - 1
                if last:
                    for copy in held_copies(n):
                        copy.wait()
                depth = len(g[1]) * widths[g[0]]
                other = jnp.concatenate(
                    [right[s, j, at : at + depth].reshape(depth * TILE, TILE) for j in range(widths[h])], 1
                )
                lanes = slice(start[g], start[g] + depth * TILE)
                part = jnp.dot(left[:, lanes], other, preferred_element_type=jnp.float32)
                if m > 0 or h in before_refs:
                    part += acc[t, :, :wide]
                if keep is None or not last:
                    acc[t, :, :wide] = part
                    continue
                for i in range(tile_rows):
                    rows = slice(i * TILE, (i + 1) * TILE)
                    for j in range(widths[h]):
                        lanes = slice(j * TILE, (j + 1) * TILE)
                        b = 2.0 * keep_cube[row + i, col + j].astype(jnp.float32)
                        rest = held[t, rows, lanes]
                        if base is None:
                            rest = 3.0 * keep_square[row + i, col + j].astype(jnp.float32) * rest
                        held[t, rows, lanes] = rest - b * part[rows, lanes]
            store(n).start()
        for n in range(max(len(hs) - 2, 0), len(hs)):
            store(n).wait()

    return pl.pallas_call(
        kernel,
        out_shape=out_shape,
        in_specs=specs,
        out_specs=[ANY] * len(out_shape),
        scratch_shapes=[
            pltpu.VMEM((nrows, total), jnp.bfloat16),
            pltpu.VMEM((2, widest, deepest, TILE, TILE), jnp.bfloat16),
            pltpu.VMEM((3, nrows, widest * TILE), jnp.float32),
            pltpu.VMEM((3, nrows, widest * TILE) if keep is not None else (3, 8, TILE), jnp.float32),
            pltpu.SemaphoreType.DMA((len(groups),)),
            pltpu.SemaphoreType.DMA((2, max(len(job) for job in jobs.values()))),
            pltpu.SemaphoreType.DMA((3,)),
            pltpu.SemaphoreType.DMA((3,)),
            pltpu.SemaphoreType.DMA((3,)),
        ],
        compiler_params=pltpu.CompilerParams(vmem_limit_bytes=VMEM_BYTES),
        cost_estimate=SMALL,
        name="cube_part",
    )(*operands)


def packed_step(density, table, place, pattern_square, pattern_cube, spans):
    nrows, ncols = density.shape
    shape = nrows // TILE, ncols // TILE
    widths = WIDTHS
    cap = spans[-1][1]
    *halves, first_chunk = pack(table, place, density, [(0, cap // 2), (cap // 2, cap), spans[0]])

    def swap(x, k):
        return lax.ppermute(x, "row", [(i, i ^ k) for i in range(ROW_GROUP)])

    def gather(x):
        return lax.all_gather(x, "col", axis=0, tiled=True)

    chunks = [gather(first_chunk)]
    by_x, by_y = [swap(x, 1) for x in halves], [swap(x, 2) for x in halves]
    chunks.append(gather(stage(halves, *spans[1], by_x + by_y)))
    far = [swap(by_x[0], 2), swap(by_y[1], 1)]
    near_part = row_unpack(table, place, density, [None, by_x, by_y], [0, 1, 2])

    lists, counts = column_lists(table, place, *shape)
    group = functools.partial(square_group, lists, counts, place)
    panels, squares, strips = [], [], []

    def send(square, low, at_once):
        squares.append(square)
        others = (1, 2, 3) if at_once else (1, 2)
        strips.append([[(low, 0)]] + [[(swap(low, k), 0)] for k in others])

    def forward(h, after=()):
        (x, _), (y, _) = strips[h][1][0], strips[h][2][0]
        top, bottom = split(x, y, after)
        strips[h].append([(swap(top, 2), 0), (swap(bottom, 1), nrows // 2)])
        return top

    near_panel, partial, _ = group([near_part], chunks[:1], spans, 0, widths[0], shape, [0, 1, 2])
    far_part = row_unpack(table, place, density, [far], [3], [partial])
    chunks.append(gather(stage(halves, *spans[2], [far_part])))
    far_panel, square, low = group([far_part], chunks[:1], spans, 0, widths[0], shape, [3], partial)
    panels.append([(near_panel, k * shape[1]) for k in range(3)] + [(far_panel, 0)])
    send(square, low, False)

    def next_group(h, at_once, after):
        parts = [near_part, far_part]
        panel, square, low = group(
            parts, chunks[: h + 1], spans, sum(widths[:h]), widths[h], shape, [0, 1, 2, 3], None, after
        )
        panels.append([(panel, k * shape[1]) for k in range(ROW_GROUP)])
        send(square, low, at_once)

    next_group(1, False, [])
    forward(0)
    chunks.append(gather(stage(halves, *spans[3], [low])))
    next_group(2, True, [forward(1)])
    every = tuple(range(ROW_GROUP))
    first, second, third = [(g, every) for g in range(3)]
    keep = place, pattern_square, pattern_cube

    def add(jobs, base=None, joined=False, after=()):
        return dict(zip(jobs, cube_part(
            strips, panels, jobs, widths, {}, keep, squares if base is None else None, base, joined, after
        )))

    parts = add({0: [first, second], 1: [first, second]}, after=[squares[2]])
    next_group(3, False, [parts[0]])
    parts.update(add({2: [first, second], 3: [first, second]}))
    parts = add({h: [third] for h in range(4)}, parts)
    forward(3, [parts[0]])
    parts = add({h: [(3, every[:3])] for h in range(4)}, parts)
    return add({h: [(3, every[3:])] for h in range(4)}, parts, True)[0]


def local(density, pattern_p, pattern_square, pattern_cube):
    tile_rows, tile_cols = density.shape[0] // TILE, density.shape[1] // TILE
    if lax.axis_size("row") != ROW_GROUP or tile_cols != sum(WIDTHS):
        return dense_step(density, pattern_p, pattern_square, pattern_cube)
    widths = WIDTHS
    table = slot_table(pattern_p, tile_rows, tile_cols)
    place = jnp.stack([lax.axis_index("col"), lax.axis_index("row")]).astype(jnp.int32)
    level, ways = len(SIGMAS), []
    for n, sigmas in reversed(list(enumerate(SIGMAS))):
        bounds = chunk_bounds(tile_rows, widths, *sigmas)
        limit = np.tile(np.repeat(bounds, widths), table.shape[1] // tile_cols)
        fits = jnp.all(table < jnp.asarray(limit, jnp.int32)[None, :])
        level = jnp.where(fits, n, level)
        spans = list(zip([0, *bounds[:-1]], bounds))
        ways.insert(0, functools.partial(
            packed_step, density, table, place, pattern_square, pattern_cube, spans
        ))
    ways.append(lambda: dense_step(density, pattern_p, pattern_square, pattern_cube))
    return lax.switch(level, ways)


def solution(mesh):
    placed = (P("col", "row"), P(), P(), P())
    return jax.shard_map(
        local, mesh=mesh, in_specs=placed, out_specs=P("col", "row"), check_vma=False
    )
```

```python
import functools
import math

import jax
import jax.numpy as jnp
import numpy as np
from jax import lax
from jax.experimental import pallas as pl
from jax.experimental.pallas import tpu as pltpu
from jax.sharding import PartitionSpec as P

TILE = 128
ROW_GROUP = 4
WIDTHS = (4, 4, 4, 4)
SIGMAS = ((3.2, 2.1), (4.2, 3.5))
SMALL = pl.CostEstimate(flops=1, bytes_accessed=1, transcendentals=0)
VMEM_BYTES = 60 * 2**20
SMEM = pl.BlockSpec(memory_space=pltpu.SMEM)
VMEM = pl.BlockSpec(memory_space=pltpu.VMEM)
ANY = pl.BlockSpec(memory_space=pl.ANY)


def tile_mask(pattern, row_start, col_start, nrows, ncols):
    tile_rows = nrows // TILE + 2
    tile_cols = ncols // TILE + 2
    padded = jnp.pad(pattern, ((0, tile_rows), (0, tile_cols)))
    block = lax.dynamic_slice(
        padded, (row_start // TILE, col_start // TILE), (tile_rows, tile_cols)
    )
    spread = jnp.repeat(jnp.repeat(block, TILE, 0), TILE, 1)
    return lax.dynamic_slice(spread, (row_start % TILE, col_start % TILE), (nrows, ncols))


def dense_step(density, pattern_p, pattern_square, pattern_cube):
    nrows, ncols = density.shape
    row_start = lax.axis_index("col") * nrows
    col_start = lax.axis_index("row") * ncols
    masked = density * tile_mask(pattern_p, row_start, col_start, nrows, ncols).astype(jnp.bfloat16)
    column_panel = lax.all_gather(masked, "col", axis=0, tiled=True)

    def right_fold(piece):
        return jnp.dot(piece, column_panel, preferred_element_type=jnp.float32)

    square = right_fold(lax.all_gather(masked, "row", axis=1, tiled=True))
    cube = right_fold(lax.all_gather(square.astype(jnp.bfloat16), "row", axis=1, tiled=True))
    keep_square = tile_mask(pattern_square, row_start, col_start, nrows, ncols).astype(jnp.float32)
    keep_cube = tile_mask(pattern_cube, row_start, col_start, nrows, ncols).astype(jnp.float32)
    return 3.0 * keep_square * square - 2.0 * keep_cube * cube


def chunk_bounds(tile_rows, widths, part_sigmas, sigmas):
    bounds, cols = [], 0
    for width in widths:
        cols += width
        tiles = tile_rows * cols
        more = (sigmas if cols == sum(widths) else part_sigmas) * math.sqrt(tiles)
        bounds.append(min(tiles, 2 * math.ceil((tiles + more) / 4)))
    return [min(b, bounds[-1]) for b in bounds]


def slot_table(pattern, tile_rows, tile_cols):
    n = pattern.shape[0]
    at = np.arange(n)
    same_rows = at[:, None] // tile_rows == at[None, :] // tile_rows
    above = (same_rows & (at[None, :] < at[:, None])).astype(np.float32)
    same_cols = at[:, None] // tile_cols == at[None, :] // tile_cols
    left = (same_cols & (at[:, None] < at[None, :])).astype(np.float32)
    kept = pattern.astype(jnp.bfloat16)
    dot = functools.partial(jnp.dot, preferred_element_type=jnp.float32)
    in_column = dot(jnp.asarray(above, jnp.bfloat16), kept)
    column = dot(jnp.asarray(same_rows, jnp.bfloat16), kept).astype(jnp.bfloat16)
    before = dot(column, jnp.asarray(left, jnp.bfloat16))
    return jnp.where(pattern != 0, (in_column + before).astype(jnp.int32), -1)


def column_lists(table, place, tile_rows, tile_cols):
    n = table.shape[0]
    blocks = n // tile_rows
    tiles = tile_rows * tile_cols
    mine = lax.dynamic_slice(table, (0, place[1] * tile_cols), (n, tile_cols)).reshape(blocks, tile_rows, tile_cols)
    order = mine.transpose(0, 2, 1).reshape(blocks, tiles, 1)
    which = lax.broadcasted_iota(jnp.int32, (blocks, tiles, tiles), 1)
    slot = lax.broadcasted_iota(jnp.int32, (blocks, tiles, tiles), 2)
    spot = which // tile_rows * n + which % tile_rows
    lists = jnp.sum(jnp.where(order == slot, spot, 0), 1)
    column = lax.broadcasted_iota(jnp.int32, (blocks, tiles, tile_cols + 1), 1) // tile_rows
    limit = lax.broadcasted_iota(jnp.int32, (blocks, tiles, tile_cols + 1), 2)
    counts = jnp.sum(jnp.where((order >= 0) & (column < limit), 1, 0), 1)
    return lists, counts


def tile_at(ref, i, j):
    return ref.at[pl.ds(pl.multiple_of(i * TILE, TILE), TILE), pl.ds(pl.multiple_of(j * TILE, TILE), TILE)]


def send_kept(table_ref, place_ref, x_ref, outs, sems, spans, shape):
    tile_rows, tile_cols = shape
    c, r = place_ref[0], place_ref[1]

    def send(i, j, slot):
        for q, (lo, hi) in enumerate(spans):
            @pl.when((slot >= lo) & (slot < hi))
            def _():
                pltpu.make_async_copy(tile_at(x_ref, i, j), outs[q].at[slot - lo], sems.at[q]).start()

    def step(n, used):
        j, i = n // tile_rows, n % tile_rows
        slot = table_ref[c * tile_rows + i, r * tile_cols + j]
        send(i, j, slot)
        return used + (slot >= 0).astype(jnp.int32)

    used = lax.fori_loop(0, tile_rows * tile_cols, step, jnp.int32(0))
    top = max(hi for _, hi in spans)

    def fill(slot, z):
        send(0, 0, slot)
        return z

    lax.fori_loop(used, jnp.int32(top), fill, 0)
    for q, out in enumerate(outs):
        pltpu.make_async_copy(out, out, sems.at[q]).wait()


def pack(table, place, density, spans, after=()):
    shape = density.shape[0] // TILE, density.shape[1] // TILE

    def kernel(table_ref, place_ref, x_ref, *refs):
        send_kept(table_ref, place_ref, x_ref, refs[len(after) : -1], refs[-1], spans, shape)

    return pl.pallas_call(
        kernel,
        out_shape=[jax.ShapeDtypeStruct((hi - lo, TILE, TILE), density.dtype) for lo, hi in spans],
        in_specs=[SMEM, SMEM, VMEM] + [ANY] * len(after),
        out_specs=[ANY] * len(spans),
        scratch_shapes=[pltpu.SemaphoreType.DMA((len(spans),))],
        name="pack",
    )(table, place, density, *after)


def stage(halves, lo, hi, after):
    cut = halves[0].shape[0]
    parts = []
    if lo < cut:
        parts.append((0, lo, min(hi, cut)))
    if hi > cut:
        parts.append((1, max(lo, cut) - cut, hi - cut))

    def kernel(h0, h1, *refs):
        out, sem = refs[-2:]
        at, copies = 0, []
        for which, first, end in parts:
            src = (h0, h1)[which].at[pl.ds(first, end - first)]
            copies.append(pltpu.make_async_copy(src, out.at[pl.ds(at, end - first)], sem.at[which]))
            at += end - first
        for copy in copies:
            copy.start()
        for copy in copies:
            copy.wait()

    return pl.pallas_call(
        kernel,
        out_shape=jax.ShapeDtypeStruct((hi - lo, TILE, TILE), halves[0].dtype),
        in_specs=[ANY] * (2 + len(after)),
        out_specs=VMEM,
        scratch_shapes=[pltpu.SemaphoreType.DMA((2,))],
        name="stage",
    )(*halves, *after)


def split(x, y, after):
    nrows, ncols = x.shape
    half = jax.ShapeDtypeStruct((nrows // 2, ncols), x.dtype)

    def kernel(x_ref, y_ref, *refs):
        top, bottom, sem = refs[-3:]
        copies = [
            pltpu.make_async_copy(x_ref.at[pl.ds(0, nrows // 2)], top, sem.at[0]),
            pltpu.make_async_copy(y_ref.at[pl.ds(nrows // 2, nrows // 2)], bottom, sem.at[1]),
        ]
        for copy in copies:
            copy.start()
        for copy in copies:
            copy.wait()

    return pl.pallas_call(
        kernel,
        out_shape=[half, half],
        in_specs=[ANY] * (2 + len(after)),
        out_specs=[VMEM, VMEM],
        scratch_shapes=[pltpu.SemaphoreType.DMA((2,))],
        name="split",
    )(x, y, *after)


def row_unpack(table, place, density, pieces, ks, after=()):
    nrows, ncols = density.shape
    tile_rows, tile_cols = nrows // TILE, ncols // TILE
    flat = [x for piece in pieces if piece is not None for x in piece]
    sizes = [x.shape[0] for x in flat[:2]]

    def kernel(table_ref, place_ref, x_ref, *refs):
        ins, (out, held, sems) = refs[: len(flat)], refs[-3:]
        i = pl.program_id(0)
        c, r = place_ref[0], place_ref[1]

        @pl.when(i == 0)
        def _():
            copies = []
            for n, ref in enumerate(ins):
                which = n % 2
                target = held.at[n // 2, pl.ds(which * sizes[0], sizes[which])]
                copies.append(pltpu.make_async_copy(ref, target, sems.at[n]))
            for copy in copies:
                copy.start()
            for copy in copies:
                copy.wait()

        at = 0
        for n, (k, piece) in enumerate(zip(ks, pieces)):
            for j in range(tile_cols):
                slot = table_ref[c * tile_rows + i, (r ^ k) * tile_cols + j]
                if piece is None:
                    tile = x_ref[:, j * TILE : (j + 1) * TILE]
                else:
                    tile = held[at, jnp.maximum(slot, 0)]
                d = n * tile_cols + j
                out[:, d * TILE : (d + 1) * TILE] = jnp.where(slot >= 0, tile, jnp.zeros_like(tile))
            at += piece is not None

    return pl.pallas_call(
        kernel,
        grid=(tile_rows,),
        out_shape=jax.ShapeDtypeStruct((nrows, len(ks) * ncols), jnp.bfloat16),
        in_specs=[SMEM, SMEM, pl.BlockSpec((TILE, ncols), lambda i: (i, 0))] + [ANY] * (len(flat) + len(after)),
        out_specs=pl.BlockSpec((TILE, len(ks) * ncols), lambda i: (i, 0)),
        scratch_shapes=[
            pltpu.VMEM((len(flat) // 2, sum(sizes), TILE, TILE), jnp.bfloat16),
            pltpu.SemaphoreType.DMA((len(flat),)),
        ],
        compiler_params=pltpu.CompilerParams(vmem_limit_bytes=VMEM_BYTES),
        cost_estimate=SMALL,
        name="row_unpack",
    )(table, place, density, *flat, *after)


def square_group(lists, counts, place, row_parts, chunks, spans, first, width, shape, ks, partial=None, after=()):
    tile_rows, tile_cols = shape
    nrows = row_parts[0].shape[0]
    span = tile_cols * TILE
    count = len(ks)
    depth = count * span
    n = width * TILE
    n_tiles = ROW_GROUP * tile_cols
    bits = (tile_cols * width).bit_length()

    def kernel(lists_ref, counts_ref, place_ref, *refs):
        a_refs, refs = refs[: len(row_parts)], refs[len(row_parts) :]
        ins, refs = refs[: len(chunks)], refs[len(chunks) :]
        if partial is not None:
            partial_ref, refs = refs[0], refs[1:]
        panel_out, square, low, a, panel, kept, a_sems, sems, out_sem, partial_sem = refs[len(after) :]
        r = place_ref[1]
        owners = tile_cols // tile_rows

        part = at = 0
        for k in range(count):
            source = a_refs[part].at[:, pl.ds(at, span)]
            pltpu.make_async_copy(source, a.at[k], a_sems.at[k]).start()
            at += span
            if at == row_parts[part].shape[1]:
                part, at = part + 1, 0
        if partial is not None:
            before = pltpu.make_async_copy(partial_ref, square, partial_sem)
            before.start()

        def fetch(k, z):
            for j in range(width):
                at = pl.ds(j * n_tiles + k * tile_cols, tile_cols)
                panel[at] = jnp.zeros((tile_cols, TILE, TILE), panel.dtype)
            total = jnp.int32(0)
            for o in range(owners):
                owner = (r ^ (k + ks[0])) * owners + o
                begin, end = counts_ref[owner, first], counts_ref[owner, first + width]
                total += end - begin
                base = k * tile_cols + o * tile_rows - first * n_tiles
                for q, (lo, hi) in enumerate(spans[: len(chunks)]):
                    shift = owner * (hi - lo) - lo

                    def one(slot, z):
                        target = panel.at[base + lists_ref[owner, slot]]
                        pltpu.make_async_copy(ins[q].at[shift + slot], target, sems.at[k]).start()
                        return z

                    lax.fori_loop(jnp.maximum(begin, lo), jnp.minimum(end, hi), one, 0)
            kept[k] = total
            return z

        lax.fori_loop(0, count, fetch, 0)

        def out_copies(k):
            rows = pl.ds(k * tile_cols, tile_cols)
            return [
                pltpu.make_async_copy(panel.at[pl.ds(j * n_tiles + k * tile_cols, tile_cols)], panel_out.at[j, rows], out_sem)
                for j in range(width)
            ]

        def multiply(k, z):
            for bit in range(bits):
                some = ins[0].at[pl.ds(0, 1 << bit)]

                @pl.when((kept[k] >> bit) & 1 == 1)
                def _():
                    pltpu.make_async_copy(some, some, sems.at[k]).wait()

            pltpu.make_async_copy(a.at[k], a.at[k], a_sems.at[k]).wait()
            for copy in out_copies(k):
                copy.start()
            right = jnp.concatenate([
                panel[pl.ds(j * n_tiles + k * tile_cols, tile_cols)].reshape(span, TILE) for j in range(width)
            ], 1)
            square[...] += jnp.dot(a[k], right, preferred_element_type=jnp.float32)
            return z

        if partial is not None:
            before.wait()
        else:
            square[...] = jnp.zeros_like(square)
        lax.fori_loop(0, count, multiply, 0)
        low[...] = square[...].astype(jnp.bfloat16)
        for k in range(count):
            for copy in out_copies(k):
                copy.wait()

    operands = [*row_parts, *chunks, *([] if partial is None else [partial]), *after]
    return pl.pallas_call(
        kernel,
        out_shape=[
            jax.ShapeDtypeStruct((width, count * tile_cols, TILE, TILE), jnp.bfloat16),
            jax.ShapeDtypeStruct((nrows, n), jnp.float32),
            jax.ShapeDtypeStruct((nrows, n), jnp.bfloat16),
        ],
        in_specs=[SMEM] * 3 + [ANY] * len(operands),
        out_specs=[ANY, VMEM, VMEM],
        scratch_shapes=[
            pltpu.VMEM((count, nrows, span), jnp.bfloat16),
            pltpu.VMEM((width * n_tiles, TILE, TILE), jnp.bfloat16),
            pltpu.SMEM((count,), jnp.int32),
            pltpu.SemaphoreType.DMA((count,)),
            pltpu.SemaphoreType.DMA((count,)),
            pltpu.SemaphoreType.DMA,
            pltpu.SemaphoreType.DMA,
        ],
        compiler_params=pltpu.CompilerParams(vmem_limit_bytes=VMEM_BYTES),
        cost_estimate=SMALL,
        name="square_group",
    )(lists, counts, place, *operands)


def cube_part(strips, panels, jobs, widths, before, keep=None, squares=None, base=None, joined=False, after=()):
    groups = sorted({g for job in jobs.values() for g, _ in job})
    firsts = [sum(widths[:h]) for h in range(len(widths))]
    tile_cols = sum(widths)
    span = tile_cols * TILE
    nrows = strips[0][0][0][0].shape[0]
    tile_rows = nrows // TILE
    lefts, start = [], {}
    at = 0
    for g in groups:
        for k in range(ROW_GROUP):
            start[g, k] = at
            lefts += [(x, row, at, (g, k)) for x, row in strips[g][k]]
            at += widths[g] * TILE
    total = at
    hs = list(jobs)
    deepest = max(sum(len(ks) * widths[g] for g, ks in job) for job in jobs.values())
    widest = max(widths[h] for h in hs)
    with_before = [h for h in hs if h in before]
    held_from = base if base is not None else squares
    operands = [x for x, *_ in lefts] + [x for h in hs for x, _ in panels[h]] + [before[h] for h in with_before]
    specs = [ANY] * len(operands)
    if keep is not None:
        operands += [*keep, *(held_from[h] for h in hs)]
        specs += [SMEM] * 3 + [ANY] * len(hs)
    operands += after
    specs += [ANY] * len(after)
    if joined:
        out_shape = [jax.ShapeDtypeStruct((nrows, span), jnp.float32)]
    else:
        out_shape = [jax.ShapeDtypeStruct((nrows, widths[h] * TILE), jnp.float32) for h in hs]

    def kernel(*refs):
        refs = list(refs)

        def take(count):
            taken = refs[:count]
            del refs[:count]
            return taken

        left_refs = take(len(lefts))
        panel_refs = {h: take(ROW_GROUP) for h in hs}
        before_refs = dict(zip(with_before, take(len(with_before))))
        if keep is not None:
            place_ref, keep_square, keep_cube = take(3)
            held_refs = dict(zip(hs, take(len(hs))))
        take(len(after))
        outs = take(len(out_shape))
        left, right, acc, held, left_sems, right_sems, acc_sems, held_sems, out_sems = refs

        def left_copies(g, k):
            sem = left_sems.at[groups.index(g) * ROW_GROUP + k]
            return [
                pltpu.make_async_copy(ref, left.at[pl.ds(row, x.shape[0]), pl.ds(at, x.shape[1])], sem)
                for ref, (x, row, at, spot) in zip(left_refs, lefts)
                if spot == (g, k)
            ]

        def right_copies(n, at, group):
            h, s = hs[n], n % 2
            g, ks = group
            copies = []
            for m, k in enumerate(ks):
                ref, shift = panel_refs[h][k], panels[h][k][1]
                copies.append(pltpu.make_async_copy(
                    ref.at[:, pl.ds(shift + firsts[g], widths[g])],
                    right.at[s, pl.ds(0, widths[h]), pl.ds(at + m * widths[g], widths[g])],
                    right_sems.at[s, jobs[h].index(group)],
                ))
            return copies

        def acc_copies(n):
            h, t = hs[n], n % 3
            lanes = pl.ds(0, widths[h] * TILE)
            copies = []
            if h in before_refs:
                copies.append(pltpu.make_async_copy(before_refs[h], acc.at[t, :, lanes], acc_sems.at[t]))
            return copies

        def held_copies(n):
            h, t = hs[n], n % 3
            lanes = pl.ds(0, widths[h] * TILE)
            copies = []
            if keep is not None:
                copies.append(pltpu.make_async_copy(held_refs[h], held.at[t, :, lanes], held_sems.at[t]))
            return copies

        def steps(h):
            at, found = 0, []
            for g in jobs[h]:
                found.append((at, g))
                at += len(g[1]) * widths[g[0]]
            return found

        def loads(n):
            copies, begun = [], set()
            for m, (at, group) in enumerate(steps(hs[n])):
                if n == 0:
                    g, ks = group
                    copies += [copy for k in ks for copy in left_copies(g, k)]
                    begun |= {(g, k) for k in ks}
                copies += right_copies(n, at, group)
                if m == 0:
                    copies += acc_copies(n)
            copies += held_copies(n)
            if n == 0:
                copies += [copy for spot in start if spot not in begun for copy in left_copies(*spot)]
            return copies

        def store(n):
            h, t = hs[n], n % 3
            lanes = pl.ds(0, widths[h] * TILE)
            source = (acc if keep is None else held).at[t, :, lanes]
            target = outs[n] if not joined else outs[0].at[:, pl.ds(firsts[h] * TILE, widths[h] * TILE)]
            return pltpu.make_async_copy(source, target, out_sems.at[t])

        for copy in loads(0):
            copy.start()
        arrived = set()
        for n, h in enumerate(hs):
            s, t, wide = n % 2, n % 3, widths[h] * TILE
            if n >= 2:
                store(n - 2).wait()
            if n + 1 < len(hs):
                for copy in loads(n + 1):
                    copy.start()
            row, col = (place_ref[0] * tile_rows, place_ref[1] * tile_cols + firsts[h]) if keep is not None else (0, 0)
            for copy in acc_copies(n):
                copy.wait()
            found = steps(h)
            for m, (at, g) in enumerate(found):
                for spot in [(g[0], k) for k in g[1] if (g[0], k) not in arrived]:
                    arrived.add(spot)
                    for copy in left_copies(*spot):
                        copy.wait()
                for copy in right_copies(n, at, g):
                    copy.wait()
                last = m == len(found) - 1
                if last:
                    for copy in held_copies(n):
                        copy.wait()
                depth = len(g[1]) * widths[g[0]]
                other = jnp.concatenate(
                    [right[s, j, at : at + depth].reshape(depth * TILE, TILE) for j in range(widths[h])], 1
                )
                lanes = slice(start[g[0], g[1][0]], start[g[0], g[1][0]] + depth * TILE)
                part = jnp.dot(left[:, lanes], other, preferred_element_type=jnp.float32)
                if m > 0 or h in before_refs:
                    part += acc[t, :, :wide]
                if keep is None or not last:
                    acc[t, :, :wide] = part
                    continue
                for i in range(tile_rows):
                    rows = slice(i * TILE, (i + 1) * TILE)
                    for j in range(widths[h]):
                        lanes = slice(j * TILE, (j + 1) * TILE)
                        b = 2.0 * keep_cube[row + i, col + j].astype(jnp.float32)
                        rest = held[t, rows, lanes]
                        if base is None:
                            rest = 3.0 * keep_square[row + i, col + j].astype(jnp.float32) * rest
                        held[t, rows, lanes] = rest - b * part[rows, lanes]
            store(n).start()
        for n in range(max(len(hs) - 2, 0), len(hs)):
            store(n).wait()

    return pl.pallas_call(
        kernel,
        out_shape=out_shape,
        in_specs=specs,
        out_specs=[ANY] * len(out_shape),
        scratch_shapes=[
            pltpu.VMEM((nrows, total), jnp.bfloat16),
            pltpu.VMEM((2, widest, deepest, TILE, TILE), jnp.bfloat16),
            pltpu.VMEM((3, nrows, widest * TILE), jnp.float32),
            pltpu.VMEM((3, nrows, widest * TILE) if keep is not None else (3, 8, TILE), jnp.float32),
            pltpu.SemaphoreType.DMA((ROW_GROUP * len(groups),)),
            pltpu.SemaphoreType.DMA((2, max(len(job) for job in jobs.values()))),
            pltpu.SemaphoreType.DMA((3,)),
            pltpu.SemaphoreType.DMA((3,)),
            pltpu.SemaphoreType.DMA((3,)),
        ],
        compiler_params=pltpu.CompilerParams(vmem_limit_bytes=VMEM_BYTES),
        cost_estimate=SMALL,
        name="cube_part",
    )(*operands)


def packed_step(density, table, place, pattern_square, pattern_cube, spans):
    nrows, ncols = density.shape
    shape = nrows // TILE, ncols // TILE
    widths = WIDTHS
    cap = spans[-1][1]
    first_chunk, = pack(table, place, density, [spans[0]])
    halves = pack(table, place, density, [(0, cap // 2), (cap // 2, cap)], [first_chunk])

    def swap(x, k):
        return lax.ppermute(x, "row", [(i, i ^ k) for i in range(ROW_GROUP)])

    def gather(x):
        return lax.all_gather(x, "col", axis=0, tiled=True)

    chunks = [gather(first_chunk)]
    by_x, by_y = [swap(x, 1) for x in halves], [swap(x, 2) for x in halves]
    chunks.append(gather(stage(halves, *spans[1], by_x + by_y)))
    far = [swap(by_x[0], 2), swap(by_y[1], 1)]
    near_part = row_unpack(table, place, density, [None, by_x, by_y], [0, 1, 2])

    lists, counts = column_lists(table, place, *shape)
    group = functools.partial(square_group, lists, counts, place)
    panels, squares, strips = [], [], []

    def send(square, low, at_once):
        squares.append(square)
        others = (1, 2, 3) if at_once else (1, 2)
        strips.append([[(low, 0)]] + [[(swap(low, k), 0)] for k in others])

    def forward(h, after=()):
        (x, _), (y, _) = strips[h][1][0], strips[h][2][0]
        top, bottom = split(x, y, after)
        strips[h].append([(swap(top, 2), 0), (swap(bottom, 1), nrows // 2)])
        return top

    near_panel, partial, _ = group([near_part], chunks[:1], spans, 0, widths[0], shape, [0, 1, 2])
    far_part = row_unpack(table, place, density, [far], [3], [partial])
    chunks.append(gather(stage(halves, *spans[2], [far_part])))
    far_panel, square, low = group([far_part], chunks[:1], spans, 0, widths[0], shape, [3], partial)
    panels.append([(near_panel, k * shape[1]) for k in range(3)] + [(far_panel, 0)])
    send(square, low, False)

    def next_group(h, at_once, after):
        parts = [near_part, far_part]
        panel, square, low = group(
            parts, chunks[: h + 1], spans, sum(widths[:h]), widths[h], shape, [0, 1, 2, 3], None, after
        )
        panels.append([(panel, k * shape[1]) for k in range(ROW_GROUP)])
        send(square, low, at_once)

    next_group(1, False, [])
    forward(0)
    chunks.append(gather(stage(halves, *spans[3], [low])))
    next_group(2, True, [forward(1)])
    every = tuple(range(ROW_GROUP))
    first, second, third = [(g, every) for g in range(3)]
    keep = place, pattern_square, pattern_cube

    def add(jobs, base=None, joined=False, after=()):
        h = next(iter(jobs))
        (g, ks), *more = jobs[h]
        jobs = {**jobs, h: [(g, ks[:2]), (g, ks[2:]), *more]}
        return dict(zip(jobs, cube_part(
            strips, panels, jobs, widths, {}, keep, squares if base is None else None, base, joined, after
        )))

    parts = add({0: [first, second], 1: [first, second]}, after=[squares[2]])
    next_group(3, False, [parts[0]])
    parts.update(add({2: [first, second], 3: [first, second]}))
    parts.update(add({0: [third], 1: [third]}, parts, after=[parts[2]]))
    sent = forward(3, [parts[0]])
    parts.update(add({2: [third], 3: [third]}, parts, after=[sent]))
    return add({h: [(3, every)] for h in range(4)}, parts, True)[0]


def local(density, pattern_p, pattern_square, pattern_cube):
    tile_rows, tile_cols = density.shape[0] // TILE, density.shape[1] // TILE
    if lax.axis_size("row") != ROW_GROUP or tile_cols != sum(WIDTHS):
        return dense_step(density, pattern_p, pattern_square, pattern_cube)
    widths = WIDTHS
    table = slot_table(pattern_p, tile_rows, tile_cols)
    place = jnp.stack([lax.axis_index("col"), lax.axis_index("row")]).astype(jnp.int32)
    level, ways = len(SIGMAS), []
    for n, sigmas in reversed(list(enumerate(SIGMAS))):
        bounds = chunk_bounds(tile_rows, widths, *sigmas)
        limit = np.tile(np.repeat(bounds, widths), table.shape[1] // tile_cols)
        fits = jnp.all(table < jnp.asarray(limit, jnp.int32)[None, :])
        level = jnp.where(fits, n, level)
        spans = list(zip([0, *bounds[:-1]], bounds))
        ways.insert(0, functools.partial(
            packed_step, density, table, place, pattern_square, pattern_cube, spans
        ))
    ways.append(lambda: dense_step(density, pattern_p, pattern_square, pattern_cube))
    return lax.switch(level, ways)


def solution(mesh):
    placed = (P("col", "row"), P(), P(), P())
    return jax.shard_map(
        local, mesh=mesh, in_specs=placed, out_specs=P("col", "row"), check_vma=False
    )
```
